32 devices in a mesh: gx: 8 (over z, x), gy: 4 (over y, core).
Axes of the slice: x: 2, y: 2, z: 4, core: 2. Of those that a mesh axis runs over, the one named last changes fastest.
Arguments:
- geometry: float32 [8, 131072], P(None, ('gx', 'gy')), may hold values from -1 to 9, as said below
- panel: bfloat16 [131072, 128], P(('gx', 'gy')), may hold values from -6 to 6
- pair_first: int32 [2048], P(('gx', 'gy')), may hold values from 0 to 7
- pair_second: int32 [2048], P(('gx', 'gy')), may hold values from 0 to 71, as said below
- pair_count: int32 [32], P(('gx', 'gy')), may hold values from 1 to 64, as said below
Outputs:
- near_product: float32 [131072, 128], P(('gx', 'gy'))
The draws below stay inside these ranges and needn't reach their ends.
Inputs may be any that keep to these rules, and one draw needn't show every extreme that they name: `geometry`: rows are x, y, z, the unit direction's three components, the length and the radius; lengths lie in 0.25 to 4, radii in 0.005 to 0.02, and a filament of the device at (ix, iy) has x in ix - 0.5 to ix + 1.5 and y in iy - 0.5 to iy + 1.5. `pair_second`: the device named by every slot lies inside the grid of devices; slots at or beyond a device's count hold arbitrary entries of the same form; pairs may repeat. `pair_count`: some device uses all 64 slots.
All inputs are finite; a program needn't handle non-finite values.
Results may differ from the reference program's by a relative error of at most 0.0032.
Values may be sent and summed in bfloat16 or wider, within the bound.
A program may use at most 128 MiB of HBM per device.

```python
import math
import jax
import jax.numpy as jnp
from jax import lax

BLOCK = 512
COLS = 128
GROUP = 8
BLK_DEV = 8
PAIR_DEV = 64
GRID_X = 8
GRID_Y = 4
FIL_DEV = 4096
FILAMENTS = 131072
PAIRS = 2048


def draw_geometry(key, part):
    subkeys = jax.random.split(key, 7)
    device_ids = jnp.arange(FILAMENTS, dtype=jnp.int32) // FIL_DEV
    dev_x = (device_ids // GRID_Y).astype(jnp.float32)
    dev_y = (device_ids % GRID_Y).astype(jnp.float32)
    draw_shape = (FILAMENTS,)
    height = 1.0
    tilt_range = 1.0
    turn_range = math.pi
    lo_len = 0.5
    hi_len = 2.0
    pos_x = dev_x + jax.random.uniform(subkeys[0], draw_shape, jnp.float32, -0.5, 1.5)
    pos_y = dev_y + jax.random.uniform(subkeys[1], draw_shape, jnp.float32, -0.5, 1.5)
    pos_z = jax.random.uniform(subkeys[2], draw_shape, jnp.float32, 0.0, height)
    lift_cos = jax.random.uniform(subkeys[3], draw_shape, jnp.float32, -tilt_range, tilt_range)
    turn_angle = jax.random.uniform(subkeys[4], draw_shape, jnp.float32, -turn_range, turn_range)
    across = jnp.sqrt(1.0 - lift_cos * lift_cos)
    dir_x = across * jnp.cos(turn_angle)
    dir_y = across * jnp.sin(turn_angle)
    length = jnp.exp(jax.random.uniform(subkeys[5], draw_shape, jnp.float32, math.log(lo_len), math.log(hi_len)))
    radius = jnp.exp(jax.random.uniform(subkeys[6], draw_shape, jnp.float32, math.log(0.005), math.log(0.02)))
    return jnp.stack([pos_x, pos_y, pos_z, dir_x, dir_y, lift_cos, length, radius]).astype(jnp.float32)


def draw_pair_second(key, part):
    subkeys = jax.random.split(key, 2)
    device_ids = jnp.arange(PAIRS, dtype=jnp.int32) // PAIR_DEV
    dev_x = device_ids // GRID_Y
    dev_y = device_ids % GRID_Y
    slot_ids = jax.random.randint(subkeys[0], (PAIRS,), 0, 9, dtype=jnp.int32)
    step_x = slot_ids // 3 - 1
    step_y = slot_ids % 3 - 1
    inside = (dev_x + step_x >= 0) & (dev_x + step_x < GRID_X) & (dev_y + step_y >= 0) & (dev_y + step_y < GRID_Y)
    slot_ids = jnp.where(inside, slot_ids, 4)
    block_ids = jax.random.randint(subkeys[1], (PAIRS,), 0, BLK_DEV, dtype=jnp.int32)
    return (slot_ids * BLK_DEV + block_ids).astype(jnp.int32)


def draw_pair_count(key, part):
    subkeys = jax.random.split(key, 2)
    device_total = GRID_X * GRID_Y
    spread_ids = jax.random.randint(subkeys[0], (device_total,), 0, 64, dtype=jnp.int32)
    counts = 1 + spread_ids * spread_ids * (PAIR_DEV - 1) // 3969
    busiest = jax.random.randint(subkeys[1], (), 0, device_total, dtype=jnp.int32)
    counts = jnp.where(jnp.arange(device_total, dtype=jnp.int32) == busiest, PAIR_DEV, counts)
    return counts.astype(jnp.int32)


def touch_ends(result, stream_key, least, high):
    index_at = [jax.random.randint(jax.random.fold_in(stream_key, axis), (), 0, length) for axis, length in enumerate(result.shape)]
    longest = result.shape.index(max(result.shape))
    beside = index_at[:longest] + [(index_at[longest] + 1) % result.shape[longest]] + index_at[longest + 1:]
    return result.at[tuple(index_at)].set(least).at[tuple(beside)].set(high)


def shard_levels(own_key, dims, cuts, least, high):
    def one(position, blocks):
        heights = jax.random.uniform(jax.random.fold_in(jax.random.fold_in(own_key, 6), position), (blocks,), jnp.float32, least / len(cuts), high / len(cuts))
        return jnp.repeat(jnp.exp(heights), dims[position] // blocks).reshape((-1,) + (1,) * (len(dims) - position - 1))

    factor_of = one(*cuts[0])
    for cut in cuts[1:]:
        factor_of = factor_of * one(*cut)
    return factor_of


def centred(key, dims, width, most, cuts=(), kind=jnp.bfloat16):
    drawn = jax.random.normal(key, dims, jnp.float32) * width
    if len(cuts) > 0:
        drawn = shard_levels(key, dims, cuts, -0.22, 0.18) * drawn
    return jnp.clip(drawn, min=-most, max=most).astype(kind)


def setup_inputs(seed: int = 0) -> dict:
    splits = jax.random.split(jax.random.key(seed), 6)
    return {
        "geometry": draw_geometry(jax.random.fold_in(splits[5], 71), 0),
        "panel": centred(splits[1], (FILAMENTS, COLS), 1.0, 6.0, ((0, 32),)),
        "pair_first": touch_ends(jax.random.randint(splits[2], (PAIRS,), 0, BLK_DEV), jax.random.fold_in(splits[2], 1), 0, BLK_DEV - 1).astype(jnp.int32),
        "pair_second": draw_pair_second(jax.random.fold_in(splits[5], 71), 0),
        "pair_count": draw_pair_count(jax.random.fold_in(splits[5], 71), 0),
    }


def make_tiles(geo_rows, geo_cols, valid_mask):
    diff_x = geo_rows[:, 0, :, None] - geo_cols[:, 0, None, :]
    diff_y = geo_rows[:, 1, :, None] - geo_cols[:, 1, None, :]
    diff_z = geo_rows[:, 2, :, None] - geo_cols[:, 2, None, :]
    reach_sum = geo_rows[:, 7, :, None] + geo_cols[:, 7, None, :]
    aligned = geo_rows[:, 3, :, None] * geo_cols[:, 3, None, :] + geo_rows[:, 4, :, None] * geo_cols[:, 4, None, :] + geo_rows[:, 5, :, None] * geo_cols[:, 5, None, :]
    weight = geo_rows[:, 6, :, None] * geo_cols[:, 6, None, :]
    spread = diff_x * diff_x + diff_y * diff_y + diff_z * diff_z + reach_sum * reach_sum
    values = BLOCK ** (-0.5) * weight * aligned / jnp.sqrt(spread)
    return (values * valid_mask[:, None, None].astype(jnp.float32)).astype(jnp.bfloat16)

def reference(geometry, panel, pair_first, pair_second, pair_count):
    margin = ((1, 1), (1, 1), (0, 0), (0, 0), (0, 0))
    geo_grid = geometry.reshape(8, GRID_X, GRID_Y, BLK_DEV, BLOCK).transpose(1, 2, 3, 0, 4)
    geo_grid = jnp.pad(geo_grid, margin)
    pan_grid = jnp.pad(panel.reshape(GRID_X, GRID_Y, BLK_DEV, BLOCK, COLS), margin)
    first_all = pair_first.reshape(GRID_X * GRID_Y, PAIR_DEV)
    second_all = pair_second.reshape(GRID_X * GRID_Y, PAIR_DEV)
    lane_ids = jnp.arange(GROUP, dtype=jnp.int32)
    centre_slot = 4 * BLK_DEV
    anchor = jnp.zeros((), jnp.int32)

    def device_step(totals, device):
        dev_x = (device // GRID_Y).astype(jnp.int32)
        dev_y = (device % GRID_Y).astype(jnp.int32)
        corner = (dev_x, dev_y, anchor, anchor, anchor)
        geo_near = lax.dynamic_slice(geo_grid, corner, (3, 3, BLK_DEV, 8, BLOCK)).reshape(9 * BLK_DEV, 8, BLOCK)
        pan_near = lax.dynamic_slice(pan_grid, corner, (3, 3, BLK_DEV, BLOCK, COLS)).reshape(9 * BLK_DEV, BLOCK, COLS)
        first_row = first_all[device]
        second_row = second_all[device]
        pair_total = pair_count[device]

        def group_step(carry_pair, group_index):
            own_rows, back_rows = carry_pair
            offset = (group_index * GROUP).astype(jnp.int32)
            first_ids = lax.dynamic_slice_in_dim(first_row, offset, GROUP)
            second_ids = lax.dynamic_slice_in_dim(second_row, offset, GROUP)
            row_ids = centre_slot + first_ids
            tiles = make_tiles(geo_near[row_ids], geo_near[second_ids], offset + lane_ids < pair_total).astype(jnp.float32)
            forward = jnp.einsum('gij,gjc->gic', tiles, pan_near[second_ids].astype(jnp.float32))
            keep_mask = (second_ids != row_ids).astype(jnp.float32)[:, None, None]
            backward = jnp.einsum('gij,gic->gjc', tiles, pan_near[row_ids].astype(jnp.float32)) * keep_mask
            return ((own_rows.at[first_ids].add(forward), back_rows.at[second_ids].add(backward)), None)
        start_pair = (jnp.zeros((BLK_DEV, BLOCK, COLS), jnp.float32), jnp.zeros((9 * BLK_DEV, BLOCK, COLS), jnp.float32))
        own_rows, back_rows = lax.scan(group_step, start_pair, jnp.arange(PAIR_DEV // GROUP, dtype=jnp.int32))[0]
        back_rows = back_rows.reshape(3, 3, BLK_DEV, BLOCK, COLS)
        shares = lax.optimization_barrier(back_rows.astype(jnp.bfloat16)).astype(jnp.float32)
        shares = shares.at[1, 1].set(own_rows + back_rows[1, 1])
        window = lax.dynamic_slice(totals, corner, (3, 3, BLK_DEV, BLOCK, COLS))
        return (lax.dynamic_update_slice(totals, window + shares, corner), None)
    totals = jnp.zeros((GRID_X + 2, GRID_Y + 2, BLK_DEV, BLOCK, COLS), jnp.float32)
    totals = lax.scan(device_step, totals, jnp.arange(GRID_X * GRID_Y, dtype=jnp.int32))[0]
    return totals[1:-1, 1:-1].reshape(GRID_X * GRID_Y * BLK_DEV * BLOCK, COLS)
```

```python
import functools

import jax
import jax.numpy as jnp
from jax import lax
from jax.experimental import pallas as pl
from jax.experimental.pallas import tpu as pltpu
from jax.sharding import PartitionSpec as P

BLOCK = 512
CHUNKS = 4
MESH = pl.DeviceIdType.MESH
VMEM_LIMIT = 56 * 1024 * 1024


def halo_kernel(nx, ny, list_ref, geo_ref, pan_ref, lists, geos, pans, x_send, x_recv, z_send, z_recv, y_send, y_recv):
    gx = lax.axis_index("gx")
    gy = lax.axis_index("gy")
    fil = pan_ref.shape[0]
    step = fil // CHUNKS
    items = CHUNKS + 2
    odd = lax.rem(gx, 2)
    partner = gx + 1 - 2 * odd
    relay_to = gx + 2 - 4 * odd
    relay_from = gx - 2 + 4 * odd
    has_to = (relay_to >= 0) & (relay_to < nx)
    has_from = (relay_from >= 0) & (relay_from < nx)
    has_up = gy + 1 < ny
    has_down = gy >= 1
    near_row = 2 - 2 * odd
    far_row = 2 * odd

    def part(k, own, row, col):
        if k == 0:
            return list_ref if own else lists.at[row * 3 + col]
        if k == 1:
            return geo_ref if own else geos.at[row * 3 + col]
        rows = pl.ds((k - 2) * step, step)
        return pan_ref.at[rows] if own else pans.at[row * 3 + col, rows]

    def x_copy(k):
        return pltpu.make_async_remote_copy(
            src_ref=part(k, True, 1, 1), dst_ref=part(k, False, far_row, 1),
            send_sem=x_send.at[k], recv_sem=x_recv.at[k],
            device_id=(partner, gy), device_id_type=MESH)

    def x_arrival(k):
        return pltpu.make_async_remote_copy(
            src_ref=part(k, True, 1, 1), dst_ref=part(k, False, near_row, 1),
            send_sem=x_send.at[k], recv_sem=x_recv.at[k],
            device_id=(partner, gy), device_id_type=MESH)

    def z_copy(k):
        return pltpu.make_async_remote_copy(
            src_ref=part(k, False, near_row, 1), dst_ref=part(k, False, far_row, 1),
            send_sem=z_send.at[k], recv_sem=z_recv.at[k],
            device_id=(relay_to, gy), device_id_type=MESH)

    def y_copy(k, kind, up):
        row = (1, near_row, far_row)[kind]
        return pltpu.make_async_remote_copy(
            src_ref=part(k, kind == 0, row, 1), dst_ref=part(k, False, row, 0 if up else 2),
            send_sem=y_send.at[kind, 1 if up else 0, k], recv_sem=y_recv.at[kind, 1 if up else 0, k],
            device_id=(gx, gy + 1 if up else gy - 1), device_id_type=MESH)

    def y_arrival(k, kind, up):
        row = (1, near_row, far_row)[kind]
        return pltpu.make_async_remote_copy(
            src_ref=part(k, kind == 0, row, 1), dst_ref=part(k, False, row, 0 if up else 2),
            send_sem=y_send.at[kind, 1 if up else 0, k], recv_sem=y_recv.at[kind, 1 if up else 0, k],
            device_id=(gx, gy - 1 if up else gy + 1), device_id_type=MESH)

    barrier = pltpu.get_barrier_semaphore()

    def greet(target, there):
        @pl.when(there)
        def _():
            pl.semaphore_signal(barrier, inc=1, device_id=target, device_id_type=MESH)

    pl.semaphore_signal(barrier, inc=1, device_id=(partner, gy), device_id_type=MESH)
    greet((relay_to, gy), has_to)
    greet((relay_from, gy), has_from)
    greet((gx, gy + 1), has_up)
    greet((gx, gy - 1), has_down)
    total = 1
    for there in (has_to, has_from, has_up, has_down):
        total = total + jnp.where(there, 1, 0)
    pl.semaphore_wait(barrier, total)

    def y_starts(k, kind):
        @pl.when(has_up)
        def _():
            y_copy(k, kind, True).start()

        @pl.when(has_down)
        def _():
            y_copy(k, kind, False).start()

    for k in range(items):
        x_copy(k).start()
        y_starts(k, 0)

    def relay(k):
        x_arrival(k).wait_recv()

        @pl.when(has_to)
        def _():
            z_copy(k).start()

        y_starts(k, 1)

    def spread(k):
        @pl.when(has_from)
        def _():
            z_copy(k).wait_recv()
            y_starts(k, 2)

    for k in range(items + 1):
        if k < items:
            relay(k)
        if k >= 1:
            spread(k - 1)

    for k in range(items):
        x_copy(k).wait_send()

        @pl.when(has_to)
        def _():
            z_copy(k).wait_send()

        for kind in range(3):
            for up, sends, gets in ((True, has_up, has_down), (False, has_down, has_up)):
                if kind == 2:
                    sends = sends & has_from
                    gets = gets & has_from

                @pl.when(sends)
                def _():
                    y_copy(k, kind, up).wait_send()

                @pl.when(gets)
                def _():
                    y_arrival(k, kind, up).wait_recv()


def product_kernel(nx, ny, list_ref, lists, geo_cols, own_feat, geo_ref, geos, pan_ref, pans,
                   out_ref, count_of, todo, cols, rows, feats, pan_all, aligned, tile, sems):
    gx = lax.axis_index("gx")
    gy = lax.axis_index("gy")
    fil, width = pan_ref.shape
    blocks = fil // BLOCK
    near = 9 * blocks
    spare = blocks * near
    sides = [(sx, sy) for sx in range(3) for sy in range(3)]

    def present(slot):
        sx, sy = sides[slot]
        there = (gx + (sx - 1) >= 0) & (gx + (sx - 1) < nx)
        return there & (gy + (sy - 1) >= 0) & (gy + (sy - 1) < ny)

    def load(slot, block):
        source = pan_ref.at[pl.ds(block * BLOCK, BLOCK)] if slot == 4 else pans.at[slot, pl.ds(block * BLOCK, BLOCK)]
        return pltpu.make_async_copy(source, pan_all.at[slot * blocks + block], sems.at[slot, block])

    for slot in range(9):
        for block in range(blocks):
            load(slot, block).start()

    def clear(i, _):
        count_of[i] = 0
        return 0

    lax.fori_loop(0, spare + 1, clear, 0, unroll=8 if (spare + 1) % 8 == 0 else 1)

    def add(a, b, wanted, n):
        where_ = jnp.where(wanted, a * near + b, spare)
        seen = count_of[where_]
        todo[n] = where_
        count_of[where_] = seen + 1
        return n + jnp.where(wanted & (seen == 0), 1, 0)

    def own_pair(s, n):
        a = list_ref[0, s]
        v = list_ref[1, s]
        n = add(a, v, v >= 0, n)
        q = v - 4 * blocks
        return add(q, 4 * blocks + a, (q >= 0) & (q < blocks) & (q != a), n)

    n = lax.fori_loop(0, list_ref[2, 0], own_pair, 0)
    for slot in range(9):
        if slot != 4:
            def their_pair(s, n, slot=slot):
                q = lists[slot, 1, s] - (8 - slot) * blocks
                return add(q, slot * blocks + lists[slot, 0, s], (q >= 0) & (q < blocks), n)

            total = jnp.where(present(slot), lists[slot, 2, 0], 0)
            n = lax.fori_loop(0, total, their_pair, n)

    for block in range(blocks):
        lines = pl.ds(block * BLOCK, BLOCK)
        for c in range(4):
            cols[c, lines, :] = jnp.broadcast_to(geo_cols[lines, c:c + 1], (BLOCK, 128))
    kind = lax.broadcasted_iota(jnp.int32, (8, BLOCK), 0)
    chosen = (kind >= 3) & (kind <= 5)

    for slot in range(9):
        def prepare(block, _, slot=slot):
            lanes = pl.ds(pl.multiple_of(block * BLOCK, BLOCK), BLOCK)
            geo = geo_ref[:, lanes] if slot == 4 else geos[slot, :, lanes]
            rows[slot * blocks + block] = geo
            value = jnp.where(chosen, geo * geo[6:7, :], 0.0)
            high = value.astype(jnp.bfloat16).astype(jnp.float32)
            low = value - high
            feats[slot * blocks + block] = jnp.concatenate(
                [high, low, high, jnp.zeros_like(high)], axis=0).astype(jnp.bfloat16)
            return 0

        lax.fori_loop(0, blocks, prepare, 0)
    out_ref[...] = jnp.zeros_like(out_ref)
    for slot in range(9):
        for block in range(blocks):
            load(slot, block).wait()

    part = 128

    def item(i, _):
        index = todo[i]
        a = index // near
        b = index - a * near
        times = count_of[index].astype(jnp.float32)
        start = a * BLOCK
        for c in range(BLOCK // part):
            first = pl.multiple_of(start + c * part, part)
            aligned[pl.ds(c * part, part), :] = jnp.dot(
                own_feat[pl.ds(first, part), :], feats[b], preferred_element_type=jnp.float32)
            for r in range(0, part, 16):
                lines = pl.ds(pl.multiple_of(first + r, 16), 16)
                here = pl.ds(c * part + r, 16)
                xi, yi, zi, ai = (cols[k, lines, :] for k in range(4))
                for l in range(0, BLOCK, 128):
                    lanes = pl.ds(l, 128)
                    dx = xi - rows[b, 0:1, lanes]
                    dy = yi - rows[b, 1:2, lanes]
                    dz = zi - rows[b, 2:3, lanes]
                    da = ai + rows[b, 7:8, lanes]
                    square = dx * dx + dy * dy + dz * dz + da * da
                    tile[here, lanes] = (aligned[here, lanes] * lax.rsqrt(square)).astype(jnp.bfloat16)
            product = jnp.dot(tile[pl.ds(c * part, part), :], pan_all[b], preferred_element_type=jnp.float32)
            out_ref[pl.ds(first, part), :] += times * product
        return 0

    lax.fori_loop(0, n, item, 0)


def shards(nx, ny, geometry, panel, pair_first, pair_second, pair_count):
    fil, width = panel.shape
    blocks = fil // BLOCK
    pair_len = pair_first.shape[0]
    long = -(-pair_len // 128) * 128
    table = jnp.zeros((8, long), jnp.int32)
    table = table.at[0, :pair_len].set(pair_first).at[1, :pair_len].set(pair_second).at[2, 0].set(pair_count[0])
    items = CHUNKS + 2
    anywhere = pl.BlockSpec(memory_space=pl.ANY)
    lists, geos, pans = pl.pallas_call(
        functools.partial(halo_kernel, nx, ny),
        out_shape=(
            jax.ShapeDtypeStruct((9, 8, long), jnp.int32),
            jax.ShapeDtypeStruct((9, 8, fil), jnp.float32),
            jax.ShapeDtypeStruct((9, fil, width), jnp.bfloat16),
        ),
        in_specs=[anywhere] * 3,
        out_specs=(anywhere,) * 3,
        scratch_shapes=[
            pltpu.SemaphoreType.DMA((items,)),
            pltpu.SemaphoreType.DMA((items,)),
            pltpu.SemaphoreType.DMA((items,)),
            pltpu.SemaphoreType.DMA((items,)),
            pltpu.SemaphoreType.DMA((3, 2, items)),
            pltpu.SemaphoreType.DMA((3, 2, items)),
        ],
        compiler_params=pltpu.CompilerParams(
            collective_id=0, has_side_effects=True, vmem_limit_bytes=VMEM_LIMIT),
        name="halo",
    )(table, geometry, panel)

    turned = geometry.T
    geo_cols = jnp.concatenate([turned[:, 0:3], turned[:, 7:8]], axis=1)
    value = jnp.pad(turned[:, 3:6] * (turned[:, 6:7] * BLOCK ** (-0.5)), ((0, 0), (3, 2)))
    high = value.astype(jnp.bfloat16)
    low = (value - high.astype(jnp.float32)).astype(jnp.bfloat16)
    own_feat = jnp.concatenate([high, high, low, jnp.zeros_like(high)], axis=1)

    vmem = pl.BlockSpec(memory_space=pltpu.VMEM)
    smem = pl.BlockSpec(memory_space=pltpu.SMEM)
    near = 9 * blocks
    return pl.pallas_call(
        functools.partial(product_kernel, nx, ny),
        out_shape=jax.ShapeDtypeStruct((fil, width), jnp.float32),
        in_specs=[smem, smem, vmem, vmem, vmem, vmem, anywhere, anywhere],
        out_specs=vmem,
        scratch_shapes=[
            pltpu.SMEM((blocks * near + 8,), jnp.int32),
            pltpu.SMEM((blocks * near + 8,), jnp.int32),
            pltpu.VMEM((4, fil, 128), jnp.float32),
            pltpu.VMEM((near, 8, BLOCK), jnp.float32),
            pltpu.VMEM((near, 32, BLOCK), jnp.bfloat16),
            pltpu.VMEM((near, BLOCK, width), jnp.bfloat16),
            pltpu.VMEM((BLOCK, BLOCK), jnp.float32),
            pltpu.VMEM((BLOCK, BLOCK), jnp.bfloat16),
            pltpu.SemaphoreType.DMA((9, blocks)),
        ],
        compiler_params=pltpu.CompilerParams(vmem_limit_bytes=VMEM_LIMIT),
        name="products",
    )(table, lists, geo_cols, own_feat, geometry, geos, panel, pans)


def solution(mesh):
    nx, ny = mesh.shape["gx"], mesh.shape["gy"]
    in_specs = (
        P(None, ("gx", "gy")),
        P(("gx", "gy"), None),
        P(("gx", "gy")),
        P(("gx", "gy")),
        P(("gx", "gy")),
    )
    out_specs = P(("gx", "gy"), None)
    return jax.shard_map(functools.partial(shards, nx, ny), mesh=mesh, in_specs=in_specs,
                         out_specs=out_specs, check_vma=False)
```

```python
import functools

import jax
import jax.numpy as jnp
from jax import lax
from jax.experimental import pallas as pl
from jax.experimental.pallas import tpu as pltpu
from jax.sharding import PartitionSpec as P

BLOCK = 512
CHUNKS = 4
PART = 128
MESH = pl.DeviceIdType.MESH
VMEM_LIMIT = 56 * 1024 * 1024


def split(value):
    high = value.astype(jnp.bfloat16).astype(jnp.float32)
    return high, value - high


def direction_rows(geo):
    kind = lax.broadcasted_iota(jnp.int32, geo.shape, 0)
    return jnp.where((kind >= 3) & (kind <= 5), geo * geo[6:7, :], 0.0)


def prepare_own(block, geo_ref, cols, own_feat):
    lanes = pl.ds(pl.multiple_of(block * BLOCK, BLOCK), BLOCK)
    geo = geo_ref[:, lanes]
    high, low = split(direction_rows(geo) * BLOCK ** (-0.5))
    blank = jnp.zeros_like(high)
    turned = jnp.concatenate([high, high, low, blank, geo] + [blank] * 11, axis=0).T
    own_feat[block] = turned[:, 0:32].astype(jnp.bfloat16)
    for c, row in enumerate((32, 33, 34, 39)):
        cols[c, block] = jnp.broadcast_to(turned[:, row:row + 1], (BLOCK, 128))


def prepare_near(block, geo, rows, feats):
    rows[block] = geo
    high, low = split(direction_rows(geo))
    feats[block] = jnp.concatenate([high, low, high, jnp.zeros_like(high)], axis=0).astype(jnp.bfloat16)


def align_part(c, a, b, own_feat, feats, aligned):
    aligned[pl.ds(c * PART, PART), :] = jnp.dot(
        own_feat[a, pl.ds(c * PART, PART), :], feats[b], preferred_element_type=jnp.float32)


def tile_part(c, a, b, cols, rows, aligned, tile):
    wide = BLOCK // 128
    xj, yj, zj, aj = (rows[b, k:k + 1, :] for k in (0, 1, 2, 7))
    for r in range(c * PART, (c + 1) * PART, 16):
        xi, yi, zi, ai = (jnp.concatenate([cols[k, a, pl.ds(r, 16), :]] * wide, axis=1) for k in range(4))
        dx = xi - xj
        dy = yi - yj
        dz = zi - zj
        da = ai + aj
        square = dx * dx + dy * dy + dz * dz + da * da
        tile[pl.ds(r, 16), :] = (aligned[pl.ds(r, 16), :] * lax.rsqrt(square)).astype(jnp.bfloat16)


def halo_kernel(nx, ny, table_ref, list_ref, geo_ref, pan_ref, lists, pans, tiles, rows, feats,
                geos, cols, own_feat, aligned0, aligned1, tile0, tile1,
                x_send, x_recv, z_send, z_recv, y_send, y_recv, out_sems):
    gx = lax.axis_index("gx")
    gy = lax.axis_index("gy")
    fil = pan_ref.shape[0]
    step = fil // CHUNKS
    items = CHUNKS + 2
    blocks = fil // BLOCK
    pairs = tiles.shape[0] // 2
    odd = lax.rem(gx, 2)
    partner = gx + 1 - 2 * odd
    relay_to = gx + 2 - 4 * odd
    relay_from = gx - 2 + 4 * odd
    has_to = (relay_to >= 0) & (relay_to < nx)
    has_from = (relay_from >= 0) & (relay_from < nx)
    has_up = gy + 1 < ny
    has_down = gy >= 1
    near_row = 2 - 2 * odd
    far_row = 2 * odd

    def part(k, own, row, col):
        if k == 0:
            return list_ref if own else lists.at[row * 3 + col]
        if k == 1:
            return geo_ref if own else geos.at[row * 3 + col]
        rows = pl.ds((k - 2) * step, step)
        return pan_ref.at[rows] if own else pans.at[row * 3 + col, rows]

    def x_copy(k):
        return pltpu.make_async_remote_copy(
            src_ref=part(k, True, 1, 1), dst_ref=part(k, False, far_row, 1),
            send_sem=x_send.at[k], recv_sem=x_recv.at[k],
            device_id=(partner, gy), device_id_type=MESH)

    def x_arrival(k):
        return pltpu.make_async_remote_copy(
            src_ref=part(k, True, 1, 1), dst_ref=part(k, False, near_row, 1),
            send_sem=x_send.at[k], recv_sem=x_recv.at[k],
            device_id=(partner, gy), device_id_type=MESH)

    def z_copy(k):
        return pltpu.make_async_remote_copy(
            src_ref=part(k, False, near_row, 1), dst_ref=part(k, False, far_row, 1),
            send_sem=z_send.at[k], recv_sem=z_recv.at[k],
            device_id=(relay_to, gy), device_id_type=MESH)

    def y_copy(k, kind, up):
        row = (1, near_row, far_row)[kind]
        return pltpu.make_async_remote_copy(
            src_ref=part(k, kind == 0, row, 1), dst_ref=part(k, False, row, 0 if up else 2),
            send_sem=y_send.at[kind, 1 if up else 0, k], recv_sem=y_recv.at[kind, 1 if up else 0, k],
            device_id=(gx, gy + 1 if up else gy - 1), device_id_type=MESH)

    def y_arrival(k, kind, up):
        row = (1, near_row, far_row)[kind]
        return pltpu.make_async_remote_copy(
            src_ref=part(k, kind == 0, row, 1), dst_ref=part(k, False, row, 0 if up else 2),
            send_sem=y_send.at[kind, 1 if up else 0, k], recv_sem=y_recv.at[kind, 1 if up else 0, k],
            device_id=(gx, gy - 1 if up else gy + 1), device_id_type=MESH)

    barrier = pltpu.get_barrier_semaphore()

    def greet(target, there):
        @pl.when(there)
        def _():
            pl.semaphore_signal(barrier, inc=1, device_id=target, device_id_type=MESH)

    pl.semaphore_signal(barrier, inc=1, device_id=(partner, gy), device_id_type=MESH)
    greet((relay_to, gy), has_to)
    greet((relay_from, gy), has_from)
    greet((gx, gy + 1), has_up)
    greet((gx, gy - 1), has_down)
    total = 1
    for there in (has_to, has_from, has_up, has_down):
        total = total + jnp.where(there, 1, 0)
    pl.semaphore_wait(barrier, total)

    def y_starts(k, kind):
        @pl.when(has_up)
        def _():
            y_copy(k, kind, True).start()

        @pl.when(has_down)
        def _():
            y_copy(k, kind, False).start()

    for k in range(2):
        x_copy(k).start()
        y_starts(k, 0)
    for k in range(2, items):
        x_copy(k).start()
    y_starts(2, 0)

    def relay(k):
        x_arrival(k).wait_recv()

        @pl.when(has_to)
        def _():
            z_copy(k).start()

        y_starts(k, 1)

    def spread(k):
        @pl.when(has_from)
        def _():
            z_copy(k).wait_recv()
            y_starts(k, 2)

    def own_block(block, _):
        prepare_own(block, geo_ref, cols, own_feat)
        lanes = pl.ds(pl.multiple_of(block * BLOCK, BLOCK), BLOCK)
        prepare_near(4 * blocks + block, geo_ref[:, lanes], rows, feats)
        return 0

    lax.fori_loop(0, blocks, own_block, 0)
    for k in range(2):
        relay(k)
    for k in range(2):
        spread(k)
    for k in range(3, items):
        y_starts(k, 0)

    def near_blocks(slot):
        def near_block(block, _):
            lanes = pl.ds(pl.multiple_of(block * BLOCK, BLOCK), BLOCK)
            prepare_near(slot * blocks + block, geos[slot, :, lanes], rows, feats)
            return 0

        lax.fori_loop(0, blocks, near_block, 0)

    near_blocks(near_row * 3 + 1)

    @pl.when(has_from)
    def _():
        near_blocks(far_row * 3 + 1)

    def y_gets(kind, up):
        gets = has_down if up else has_up
        return gets & has_from if kind == 2 else gets

    for kind in range(3):
        for up in (True, False):
            @pl.when(y_gets(kind, up))
            def _():
                y_arrival(1, kind, up).wait_recv()
                near_blocks((1, near_row, far_row)[kind] * 3 + (0 if up else 2))

    def slot_ids(s):
        return list_ref[0, s], list_ref[1, s]

    def out_copy(which, tile, s):
        return pltpu.make_async_copy(tile, tiles.at[s], out_sems.at[which])

    a0, b0 = slot_ids(0)
    for c in range(BLOCK // PART):
        align_part(c, a0, b0, own_feat, feats, aligned0)

    events = {}
    for c, at in enumerate((1, 6, 11, 17)):
        events.setdefault(at * pairs // 32, []).append((relay, c + 2))
    for c, at in enumerate((6, 11, 17, 23)):
        events.setdefault(at * pairs // 32, []).append((spread, c + 2))

    def pair_step(i, _):
        for at, calls in events.items():
            @pl.when(i == at)
            def _():
                for call, k in calls:
                    call(k)

        for half, now, later, tile in ((0, aligned0, aligned1, tile0), (1, aligned1, aligned0, tile1)):
            s = 2 * i + half
            a, b = slot_ids(s)
            a_next, b_next = slot_ids(jnp.minimum(s + 1, 2 * pairs - 1))

            @pl.when(i > 0)
            def _():
                out_copy(half, tile, s).wait()

            for c in range(BLOCK // PART):
                align_part(c, a_next, b_next, own_feat, feats, later)
                tile_part(c, a, b, cols, rows, now, tile)
            out_copy(half, tile, s).start()
        return 0

    lax.fori_loop(0, pairs, pair_step, 0)
    out_copy(0, tile0, 2 * pairs - 2).wait()
    out_copy(1, tile1, 2 * pairs - 1).wait()

    for k in range(items):
        x_copy(k).wait_send()

        @pl.when(has_to)
        def _():
            z_copy(k).wait_send()

        for kind in range(3):
            for up, sends, gets in ((True, has_up, has_down), (False, has_down, has_up)):
                if kind == 2:
                    sends = sends & has_from
                    gets = gets & has_from

                @pl.when(sends)
                def _():
                    y_copy(k, kind, up).wait_send()

                if k != 1:
                    @pl.when(gets)
                    def _():
                        y_arrival(k, kind, up).wait_recv()


def product_kernel(nx, ny, list_ref, lists, geo_ref, rows, feats, pan_ref, pans, tiles,
                   out_ref, count_of, todo, slot_of, cols, own_feat, pan_all, aligned0, aligned1,
                   tile0, tile1, stored, sems, stored_sems):
    gx = lax.axis_index("gx")
    gy = lax.axis_index("gy")
    fil, width = pan_ref.shape
    blocks = fil // BLOCK
    near = 9 * blocks
    spare = blocks * near
    sides = [(sx, sy) for sx in range(3) for sy in range(3)]

    def present(slot):
        sx, sy = sides[slot]
        there = (gx + (sx - 1) >= 0) & (gx + (sx - 1) < nx)
        return there & (gy + (sy - 1) >= 0) & (gy + (sy - 1) < ny)

    def load(slot, block):
        source = pan_ref.at[pl.ds(block * BLOCK, BLOCK)] if slot == 4 else pans.at[slot, pl.ds(block * BLOCK, BLOCK)]
        return pltpu.make_async_copy(source, pan_all.at[slot * blocks + block], sems.at[slot, block])

    for slot in (4, 0, 1, 2, 3, 5, 6, 7, 8):
        for block in range(blocks):
            load(slot, block).start()

    def clear(i, _):
        count_of[i] = 0
        return 0

    lax.fori_loop(0, spare + 1, clear, 0, unroll=8 if (spare + 1) % 8 == 0 else 1)

    def add(a, b, wanted, n):
        where_ = jnp.where(wanted, a * near + b, spare)
        seen = count_of[where_]
        todo[n] = where_
        count_of[where_] = seen + 1
        return n + jnp.where(wanted & (seen == 0), 1, 0)

    def own_pair(s, n):
        slot_of[n] = s
        return add(list_ref[0, s], list_ref[1, s], True, n)

    ready = lax.fori_loop(0, list_ref[2, 0], own_pair, 0)
    depth = stored.shape[0]

    def fetch(i):
        slot = lax.rem(i, depth)
        return pltpu.make_async_copy(tiles.at[slot_of[i]], stored.at[slot], stored_sems.at[slot])

    for i in range(depth):
        @pl.when(i < ready)
        def _():
            fetch(i).start()

    def mirrored(s, n):
        q = list_ref[1, s] - 4 * blocks
        a = list_ref[0, s]
        return add(q, 4 * blocks + a, (q >= 0) & (q < blocks) & (q != a), n)

    n = lax.fori_loop(0, list_ref[2, 0], mirrored, ready)
    for slot in range(9):
        if slot != 4:
            def their_pair(s, n, slot=slot):
                q = lists[slot, 1, s] - (8 - slot) * blocks
                return add(q, slot * blocks + lists[slot, 0, s], (q >= 0) & (q < blocks), n)

            total = jnp.where(present(slot), lists[slot, 2, 0], 0)
            n = lax.fori_loop(0, total, their_pair, n)

    def own_block(block, _):
        prepare_own(block, geo_ref, cols, own_feat)
        return 0

    lax.fori_loop(0, blocks, own_block, 0)
    out_ref[...] = jnp.zeros_like(out_ref)
    for slot in range(9):
        for block in range(blocks):
            load(slot, block).wait()

    def entry(i):
        inside = i < n
        index = jnp.where(inside, todo[jnp.where(inside, i, 0)], 4 * blocks)
        a = index // near
        return a, index - a * near, jnp.where(inside, count_of[index], 0).astype(jnp.float32)

    def product_part(c, a, b, times, tile):
        first = pl.multiple_of(a * BLOCK + c * PART, PART)
        product = jnp.dot(tile[pl.ds(c * PART, PART), :], pan_all[b], preferred_element_type=jnp.float32)
        out_ref[pl.ds(first, PART), :] += times * product

    def ready_item(i, _):
        a, b, times = entry(i)
        fetch(i).wait()
        for c in range(BLOCK // PART):
            product_part(c, a, b, times, stored.at[lax.rem(i, depth)])

        @pl.when(i + depth < ready)
        def _():
            fetch(i + depth).start()

        return 0

    lax.fori_loop(0, ready, ready_item, 0)

    @pl.when(n > ready)
    def _():
        a0, b0, _ = entry(ready)
        for c in range(BLOCK // PART):
            align_part(c, a0, b0, own_feat, feats, aligned0)
        tile1[...] = jnp.zeros_like(tile1)

        def two_items(j, before):
            i = ready + 2 * j
            for half, now, later, tile, past in (
                (0, aligned0, aligned1, tile0, tile1), (1, aligned1, aligned0, tile1, tile0)):
                a, b, times = entry(i + half)
                a_next, b_next, _ = entry(i + half + 1)
                for c in range(BLOCK // PART):
                    align_part(c, a_next, b_next, own_feat, feats, later)
                    tile_part(c, a, b, cols, rows, now, tile)
                    product_part(c, *before, past)
                before = (a, b, times)
            return before

        last = lax.fori_loop(0, (n - ready + 1) // 2, two_items, (jnp.int32(0), jnp.int32(4 * blocks), jnp.float32(0)))
        for c in range(BLOCK // PART):
            product_part(c, *last, tile1)


def shards(nx, ny, geometry, panel, pair_first, pair_second, pair_count):
    fil, width = panel.shape
    blocks = fil // BLOCK
    near = 9 * blocks
    pair_len = pair_first.shape[0]
    long = -(-pair_len // 128) * 128
    made = 2 * (-(-pair_len // 2))
    table = jnp.pad(jnp.stack([pair_first, pair_second, jnp.broadcast_to(pair_count, (pair_len,))]),
                    ((0, 5), (0, long - pair_len)))
    items = CHUNKS + 2
    anywhere = pl.BlockSpec(memory_space=pl.ANY)
    vmem = pl.BlockSpec(memory_space=pltpu.VMEM)
    smem = pl.BlockSpec(memory_space=pltpu.SMEM)
    square = (BLOCK, BLOCK)
    lists, pans, tiles, rows, feats = pl.pallas_call(
        functools.partial(halo_kernel, nx, ny),
        out_shape=(
            jax.ShapeDtypeStruct((9, 8, long), jnp.int32),
            jax.ShapeDtypeStruct((9, fil, width), jnp.bfloat16),
            jax.ShapeDtypeStruct((made,) + square, jnp.bfloat16),
            jax.ShapeDtypeStruct((near, 8, BLOCK), jnp.float32),
            jax.ShapeDtypeStruct((near, 32, BLOCK), jnp.bfloat16),
        ),
        in_specs=[anywhere, smem, vmem, anywhere],
        out_specs=(anywhere, anywhere, anywhere, vmem, vmem),
        scratch_shapes=[
            pltpu.VMEM((9, 8, fil), jnp.float32),
            pltpu.VMEM((4, blocks, BLOCK, 128), jnp.float32),
            pltpu.VMEM((blocks, BLOCK, 32), jnp.bfloat16),
            pltpu.VMEM(square, jnp.float32),
            pltpu.VMEM(square, jnp.float32),
            pltpu.VMEM(square, jnp.bfloat16),
            pltpu.VMEM(square, jnp.bfloat16),
            pltpu.SemaphoreType.DMA((items,)),
            pltpu.SemaphoreType.DMA((items,)),
            pltpu.SemaphoreType.DMA((items,)),
            pltpu.SemaphoreType.DMA((items,)),
            pltpu.SemaphoreType.DMA((3, 2, items)),
            pltpu.SemaphoreType.DMA((3, 2, items)),
            pltpu.SemaphoreType.DMA((2,)),
        ],
        compiler_params=pltpu.CompilerParams(
            collective_id=0, has_side_effects=True, vmem_limit_bytes=VMEM_LIMIT),
        name="halo",
    )(table, table, geometry, panel)

    depth = 4
    return pl.pallas_call(
        functools.partial(product_kernel, nx, ny),
        out_shape=jax.ShapeDtypeStruct((fil, width), jnp.float32),
        in_specs=[smem, smem, vmem, vmem, vmem, anywhere, anywhere, anywhere],
        out_specs=vmem,
        scratch_shapes=[
            pltpu.SMEM((blocks * near + 8,), jnp.int32),
            pltpu.SMEM((blocks * near + 8,), jnp.int32),
            pltpu.SMEM((blocks * near + 8,), jnp.int32),
            pltpu.VMEM((4, blocks, BLOCK, 128), jnp.float32),
            pltpu.VMEM((blocks, BLOCK, 32), jnp.bfloat16),
            pltpu.VMEM((near, BLOCK, width), jnp.bfloat16),
            pltpu.VMEM(square, jnp.float32),
            pltpu.VMEM(square, jnp.float32),
            pltpu.VMEM(square, jnp.bfloat16),
            pltpu.VMEM(square, jnp.bfloat16),
            pltpu.VMEM((depth,) + square, jnp.bfloat16),
            pltpu.SemaphoreType.DMA((9, blocks)),
            pltpu.SemaphoreType.DMA((depth,)),
        ],
        compiler_params=pltpu.CompilerParams(vmem_limit_bytes=VMEM_LIMIT),
        name="products",
    )(table, lists, geometry, rows, feats, panel, pans, tiles)


def solution(mesh):
    nx, ny = mesh.shape["gx"], mesh.shape["gy"]
    in_specs = (
        P(None, ("gx", "gy")),
        P(("gx", "gy"), None),
        P(("gx", "gy")),
        P(("gx", "gy")),
        P(("gx", "gy")),
    )
    out_specs = P(("gx", "gy"), None)
    return jax.shard_map(functools.partial(shards, nx, ny), mesh=mesh, in_specs=in_specs,
                         out_specs=out_specs, check_vma=False)
```

```python
import functools

import jax
import jax.numpy as jnp
from jax import lax
from jax.experimental import pallas as pl
from jax.experimental.pallas import tpu as pltpu
from jax.sharding import PartitionSpec as P

BLOCK = 512
CHUNKS = 4
PART = 256
GRID = 16.0
MESH = pl.DeviceIdType.MESH
VMEM_LIMIT = 56 * 1024 * 1024


def split(value):
    high = value.astype(jnp.bfloat16).astype(jnp.float32)
    return high, value - high


def features(geo, gx, gy, own):
    kind = lax.broadcasted_iota(jnp.int32, geo.shape, 0)
    place = kind < 3
    centre = jnp.where(kind == 0, gx.astype(jnp.float32) + 0.5, jnp.where(kind == 1, gy.astype(jnp.float32) + 0.5, 4.0))
    local = geo - centre
    coarse = jnp.where(place, jnp.floor(local * GRID + 0.5) * (1.0 / GRID), 0.0)
    fine = jnp.where(place, local - coarse, 0.0)
    radius = jnp.where(kind == 7, geo, 0.0)
    fine_high, rest = split(fine)
    fine_mid, fine_low = split(rest)
    both_high, both_low = split(fine + radius)
    norm = jnp.broadcast_to(jnp.sum(coarse * coarse, axis=0, keepdims=True), geo.shape)
    extra = jnp.broadcast_to(jnp.sum((2.0 * coarse + fine) * fine + radius * radius, axis=0, keepdims=True), geo.shape)
    norm_high, norm_low = split(norm)
    extra_high, rest = split(extra)
    extra_mid, extra_low = split(rest)
    direction = jnp.where((kind >= 3) & (kind <= 5), geo * geo[6:7, :], 0.0)
    blank = jnp.zeros_like(geo)
    if own:
        high, low = split(direction * BLOCK ** (-0.5))
        norms = jnp.where(kind == 0, norm_high, jnp.where(kind == 1, norm_low, jnp.where(kind <= 3, 1.0, 0.0)))
        extras = jnp.where(kind == 0, extra_high, jnp.where(kind == 1, extra_mid, jnp.where(
            kind == 2, extra_low, jnp.where(kind <= 5, 1.0, 0.0))))
        groups = [high, high, low, blank, coarse, norms, both_high, both_high, both_low,
                  coarse, coarse, coarse, fine_high, fine_mid, fine_low, extras]
    else:
        high, low = split(direction)
        sign = jnp.where(place, -2.0, 2.0)
        norms = jnp.where(kind <= 1, 1.0, jnp.where(kind == 2, norm_high, jnp.where(kind == 3, norm_low, 0.0)))
        extras = jnp.where(kind <= 2, 1.0, jnp.where(kind == 3, extra_high, jnp.where(
            kind == 4, extra_mid, jnp.where(kind == 5, extra_low, 0.0))))
        double = -2.0 * coarse
        groups = [high, low, high, blank, double, norms, sign * both_high, sign * both_low, sign * both_high,
                  -2.0 * fine_high, -2.0 * fine_mid, -2.0 * fine_low, double, double, double, extras]
    return jnp.concatenate(groups, axis=0)


def prepare_own(block, geo_ref, gx, gy, own_along, own_coarse, own_fine):
    lanes = pl.ds(pl.multiple_of(block * BLOCK, BLOCK), BLOCK)
    turned = features(geo_ref[:, lanes], gx, gy, True).T.astype(jnp.bfloat16)
    own_along[block] = turned[:, 0:32]
    own_coarse[block] = turned[:, 32:48]
    own_fine[block] = turned[:, 48:128]


def align_part(c, a, b, own, feats, work):
    own_along, own_coarse, own_fine = own
    aligned, square = work
    here = pl.ds(c * PART, PART)
    aligned[here, :] = jnp.dot(own_along[a, here, :], feats[b, 0:32, :], preferred_element_type=jnp.float32)
    square[here, :] = jnp.dot(
        own_coarse[a, here, :], feats[b, 32:48, :], preferred_element_type=jnp.float32
    ) + jnp.dot(own_fine[a, here, :], feats[b, 48:128, :], preferred_element_type=jnp.float32)


def tile_part(c, work, tile):
    aligned, square = work
    for r in range(c * PART, (c + 1) * PART, 16):
        here = pl.ds(r, 16)
        tile[here, :] = (aligned[here, :] * lax.rsqrt(square[here, :])).astype(jnp.bfloat16)


def halo_kernel(nx, ny, table_ref, list_ref, geo_ref, pan_ref, lists, pans, tiles, feats,
                geos, own_along, own_coarse, own_fine, aligned0, aligned1, square0, square1, tile0, tile1,
                x_send, x_recv, z_send, z_recv, y_send, y_recv, out_sems):
    own = own_along, own_coarse, own_fine
    work0, work1 = (aligned0, square0), (aligned1, square1)
    gx = lax.axis_index("gx")
    gy = lax.axis_index("gy")
    fil = pan_ref.shape[0]
    step = fil // CHUNKS
    items = CHUNKS + 2
    blocks = fil // BLOCK
    pairs = tiles.shape[0] // 2
    odd = lax.rem(gx, 2)
    partner = gx + 1 - 2 * odd
    relay_to = gx + 2 - 4 * odd
    relay_from = gx - 2 + 4 * odd
    has_to = (relay_to >= 0) & (relay_to < nx)
    has_from = (relay_from >= 0) & (relay_from < nx)
    has_up = gy + 1 < ny
    has_down = gy >= 1
    near_row = 2 - 2 * odd
    far_row = 2 * odd

    def part(k, own, row, col):
        if k == 0:
            return list_ref if own else lists.at[row * 3 + col]
        if k == 1:
            return geo_ref if own else geos.at[row * 3 + col]
        rows = pl.ds((k - 2) * step, step)
        return pan_ref.at[rows] if own else pans.at[row * 3 + col, rows]

    def x_copy(k):
        return pltpu.make_async_remote_copy(
            src_ref=part(k, True, 1, 1), dst_ref=part(k, False, far_row, 1),
            send_sem=x_send.at[k], recv_sem=x_recv.at[k],
            device_id=(partner, gy), device_id_type=MESH)

    def x_arrival(k):
        return pltpu.make_async_remote_copy(
            src_ref=part(k, True, 1, 1), dst_ref=part(k, False, near_row, 1),
            send_sem=x_send.at[k], recv_sem=x_recv.at[k],
            device_id=(partner, gy), device_id_type=MESH)

    def z_copy(k):
        return pltpu.make_async_remote_copy(
            src_ref=part(k, False, near_row, 1), dst_ref=part(k, False, far_row, 1),
            send_sem=z_send.at[k], recv_sem=z_recv.at[k],
            device_id=(relay_to, gy), device_id_type=MESH)

    def y_copy(k, kind, up):
        row = (1, near_row, far_row)[kind]
        return pltpu.make_async_remote_copy(
            src_ref=part(k, kind == 0, row, 1), dst_ref=part(k, False, row, 0 if up else 2),
            send_sem=y_send.at[kind, 1 if up else 0, k], recv_sem=y_recv.at[kind, 1 if up else 0, k],
            device_id=(gx, gy + 1 if up else gy - 1), device_id_type=MESH)

    def y_arrival(k, kind, up):
        row = (1, near_row, far_row)[kind]
        return pltpu.make_async_remote_copy(
            src_ref=part(k, kind == 0, row, 1), dst_ref=part(k, False, row, 0 if up else 2),
            send_sem=y_send.at[kind, 1 if up else 0, k], recv_sem=y_recv.at[kind, 1 if up else 0, k],
            device_id=(gx, gy - 1 if up else gy + 1), device_id_type=MESH)

    barrier = pltpu.get_barrier_semaphore()

    def greet(target, there):
        @pl.when(there)
        def _():
            pl.semaphore_signal(barrier, inc=1, device_id=target, device_id_type=MESH)

    pl.semaphore_signal(barrier, inc=1, device_id=(partner, gy), device_id_type=MESH)
    greet((relay_to, gy), has_to)
    greet((relay_from, gy), has_from)
    greet((gx, gy + 1), has_up)
    greet((gx, gy - 1), has_down)
    total = 1
    for there in (has_to, has_from, has_up, has_down):
        total = total + jnp.where(there, 1, 0)
    pl.semaphore_wait(barrier, total)

    def y_starts(k, kind):
        @pl.when(has_up)
        def _():
            y_copy(k, kind, True).start()

        @pl.when(has_down)
        def _():
            y_copy(k, kind, False).start()

    for k in range(2):
        x_copy(k).start()
        y_starts(k, 0)
    for k in range(2, items):
        x_copy(k).start()
    y_starts(2, 0)

    def relay(k):
        x_arrival(k).wait_recv()

        @pl.when(has_to)
        def _():
            z_copy(k).start()

        y_starts(k, 1)

    def spread(k):
        @pl.when(has_from)
        def _():
            z_copy(k).wait_recv()
            y_starts(k, 2)

    def own_block(block, _):
        prepare_own(block, geo_ref, gx, gy, *own)
        lanes = pl.ds(pl.multiple_of(block * BLOCK, BLOCK), BLOCK)
        feats[4 * blocks + block] = features(geo_ref[:, lanes], gx, gy, False).astype(jnp.bfloat16)
        return 0

    lax.fori_loop(0, blocks, own_block, 0)
    for k in range(2):
        relay(k)
    for k in range(2):
        spread(k)
    for k in range(3, items):
        y_starts(k, 0)

    def near_blocks(slot):
        def near_block(block, _):
            lanes = pl.ds(pl.multiple_of(block * BLOCK, BLOCK), BLOCK)
            feats[slot * blocks + block] = features(geos[slot, :, lanes], gx, gy, False).astype(jnp.bfloat16)
            return 0

        lax.fori_loop(0, blocks, near_block, 0)

    near_blocks(near_row * 3 + 1)

    @pl.when(has_from)
    def _():
        near_blocks(far_row * 3 + 1)

    def y_gets(kind, up):
        gets = has_down if up else has_up
        return gets & has_from if kind == 2 else gets

    for kind in range(3):
        for up in (True, False):
            @pl.when(y_gets(kind, up))
            def _():
                y_arrival(1, kind, up).wait_recv()
                near_blocks((1, near_row, far_row)[kind] * 3 + (0 if up else 2))

    def slot_ids(s):
        return list_ref[0, s], list_ref[1, s]

    def out_copy(which, tile, s):
        return pltpu.make_async_copy(tile, tiles.at[s], out_sems.at[which])

    a0, b0 = slot_ids(0)
    for c in range(BLOCK // PART):
        align_part(c, a0, b0, own, feats, work0)

    events = {}
    for c, at in enumerate((1, 6, 11, 17)):
        events.setdefault(at * pairs // 32, []).append((relay, c + 2))
    for c, at in enumerate((6, 11, 17, 23)):
        events.setdefault(at * pairs // 32, []).append((spread, c + 2))

    def pair_step(i, _):
        for at, calls in events.items():
            @pl.when(i == at)
            def _():
                for call, k in calls:
                    call(k)

        for half, now, later, tile in ((0, work0, work1, tile0), (1, work1, work0, tile1)):
            s = 2 * i + half
            a_next, b_next = slot_ids(jnp.minimum(s + 1, 2 * pairs - 1))

            @pl.when(i > 0)
            def _():
                out_copy(half, tile, s).wait()

            for c in range(BLOCK // PART):
                align_part(c, a_next, b_next, own, feats, later)
                tile_part(c, now, tile)
            out_copy(half, tile, s).start()
        return 0

    lax.fori_loop(0, pairs, pair_step, 0)
    out_copy(0, tile0, 2 * pairs - 2).wait()
    out_copy(1, tile1, 2 * pairs - 1).wait()

    for k in range(items):
        x_copy(k).wait_send()

        @pl.when(has_to)
        def _():
            z_copy(k).wait_send()

        for kind in range(3):
            for up, sends, gets in ((True, has_up, has_down), (False, has_down, has_up)):
                if kind == 2:
                    sends = sends & has_from
                    gets = gets & has_from

                @pl.when(sends)
                def _():
                    y_copy(k, kind, up).wait_send()

                if k != 1:
                    @pl.when(gets)
                    def _():
                        y_arrival(k, kind, up).wait_recv()


def product_kernel(nx, ny, list_ref, lists, geo_ref, feats_ref, pan_ref, pans, tiles,
                   out_ref, count_of, todo, slot_of, own_along, own_coarse, own_fine, feats, pan_all,
                   aligned0, aligned1, square0, square1, tile0, tile1, stored, sems, stored_sems, feat_sem):
    own = own_along, own_coarse, own_fine
    work0, work1 = (aligned0, square0), (aligned1, square1)
    gx = lax.axis_index("gx")
    gy = lax.axis_index("gy")
    fil, width = pan_ref.shape
    blocks = fil // BLOCK
    near = 9 * blocks
    spare = blocks * near
    sides = [(sx, sy) for sx in range(3) for sy in range(3)]

    def present(slot):
        sx, sy = sides[slot]
        there = (gx + (sx - 1) >= 0) & (gx + (sx - 1) < nx)
        return there & (gy + (sy - 1) >= 0) & (gy + (sy - 1) < ny)

    def load(slot, block):
        source = pan_ref.at[pl.ds(block * BLOCK, BLOCK)] if slot == 4 else pans.at[slot, pl.ds(block * BLOCK, BLOCK)]
        return pltpu.make_async_copy(source, pan_all.at[slot * blocks + block], sems.at[slot, block])

    feat_load = pltpu.make_async_copy(feats_ref, feats, feat_sem)
    for slot in (4, 0, 1, 2, 3, 5, 6, 7, 8):
        for block in range(blocks):
            load(slot, block).start()
    feat_load.start()

    def clear(i, _):
        count_of[i] = 0
        return 0

    lax.fori_loop(0, spare + 1, clear, 0, unroll=8 if (spare + 1) % 8 == 0 else 1)

    def add(a, b, wanted, n):
        where_ = jnp.where(wanted, a * near + b, spare)
        seen = count_of[where_]
        todo[n] = where_
        count_of[where_] = seen + 1
        return n + jnp.where(wanted & (seen == 0), 1, 0)

    def own_pair(s, n):
        slot_of[n] = s
        return add(list_ref[0, s], list_ref[1, s], True, n)

    ready = lax.fori_loop(0, list_ref[2, 0], own_pair, 0)
    depth = stored.shape[0]

    def fetch(i):
        slot = lax.rem(i, depth)
        return pltpu.make_async_copy(tiles.at[slot_of[i]], stored.at[slot], stored_sems.at[slot])

    for i in range(depth):
        @pl.when(i < ready)
        def _():
            fetch(i).start()

    def mirrored(s, n):
        q = list_ref[1, s] - 4 * blocks
        a = list_ref[0, s]
        return add(q, 4 * blocks + a, (q >= 0) & (q < blocks) & (q != a), n)

    n = lax.fori_loop(0, list_ref[2, 0], mirrored, ready)
    for slot in range(9):
        if slot != 4:
            def their_pair(s, n, slot=slot):
                q = lists[slot, 1, s] - (8 - slot) * blocks
                return add(q, slot * blocks + lists[slot, 0, s], (q >= 0) & (q < blocks), n)

            total = jnp.where(present(slot), lists[slot, 2, 0], 0)
            n = lax.fori_loop(0, total, their_pair, n)

    def own_block(block, _):
        prepare_own(block, geo_ref, gx, gy, *own)
        return 0

    lax.fori_loop(0, blocks, own_block, 0)
    out_ref[...] = jnp.zeros_like(out_ref)
    for slot in range(9):
        for block in range(blocks):
            load(slot, block).wait()

    def entry(i):
        inside = i < n
        index = jnp.where(inside, todo[jnp.where(inside, i, 0)], 4 * blocks)
        a = index // near
        return a, index - a * near, jnp.where(inside, count_of[index], 0).astype(jnp.float32)

    def product_part(c, a, b, times, tile):
        first = pl.multiple_of(a * BLOCK + c * PART, PART)
        product = jnp.dot(tile[pl.ds(c * PART, PART), :], pan_all[b], preferred_element_type=jnp.float32)
        out_ref[pl.ds(first, PART), :] += times * product

    def ready_item(i, _):
        a, b, times = entry(i)
        fetch(i).wait()
        for c in range(BLOCK // PART):
            product_part(c, a, b, times, stored.at[lax.rem(i, depth)])

        @pl.when(i + depth < ready)
        def _():
            fetch(i + depth).start()

        return 0

    lax.fori_loop(0, ready, ready_item, 0)
    feat_load.wait()

    @pl.when(n > ready)
    def _():
        a0, b0, _ = entry(ready)
        for c in range(BLOCK // PART):
            align_part(c, a0, b0, own, feats, work0)
        tile1[...] = jnp.zeros_like(tile1)

        def two_items(j, before):
            i = ready + 2 * j
            for half, now, later, tile, past in (
                (0, work0, work1, tile0, tile1), (1, work1, work0, tile1, tile0)):
                a, b, times = entry(i + half)
                a_next, b_next, _ = entry(i + half + 1)
                for c in range(BLOCK // PART):
                    align_part(c, a_next, b_next, own, feats, later)
                    tile_part(c, now, tile)
                    product_part(c, *before, past)
                before = (a, b, times)
            return before

        last = lax.fori_loop(0, (n - ready + 1) // 2, two_items, (jnp.int32(0), jnp.int32(4 * blocks), jnp.float32(0)))
        for c in range(BLOCK // PART):
            product_part(c, *last, tile1)


def shards(nx, ny, geometry, panel, pair_first, pair_second, pair_count):
    fil, width = panel.shape
    blocks = fil // BLOCK
    near = 9 * blocks
    pair_len = pair_first.shape[0]
    long = -(-pair_len // 128) * 128
    made = 2 * (-(-pair_len // 2))
    table = jnp.pad(jnp.stack([pair_first, pair_second, jnp.broadcast_to(pair_count, (pair_len,))]),
                    ((0, 5), (0, long - pair_len)))
    items = CHUNKS + 2
    anywhere = pl.BlockSpec(memory_space=pl.ANY)
    vmem = pl.BlockSpec(memory_space=pltpu.VMEM)
    smem = pl.BlockSpec(memory_space=pltpu.SMEM)
    square = (BLOCK, BLOCK)
    lists, pans, tiles, feats = pl.pallas_call(
        functools.partial(halo_kernel, nx, ny),
        out_shape=(
            jax.ShapeDtypeStruct((9, 8, long), jnp.int32),
            jax.ShapeDtypeStruct((9, fil, width), jnp.bfloat16),
            jax.ShapeDtypeStruct((made,) + square, jnp.bfloat16),
            jax.ShapeDtypeStruct((near, 128, BLOCK), jnp.bfloat16),
        ),
        in_specs=[anywhere, smem, vmem, anywhere],
        out_specs=(anywhere, anywhere, anywhere, vmem),
        scratch_shapes=[
            pltpu.VMEM((9, 8, fil), jnp.float32),
            pltpu.VMEM((blocks, BLOCK, 32), jnp.bfloat16),
            pltpu.VMEM((blocks, BLOCK, 16), jnp.bfloat16),
            pltpu.VMEM((blocks, BLOCK, 80), jnp.bfloat16),
            pltpu.VMEM(square, jnp.float32),
            pltpu.VMEM(square, jnp.float32),
            pltpu.VMEM(square, jnp.float32),
            pltpu.VMEM(square, jnp.float32),
            pltpu.VMEM(square, jnp.bfloat16),
            pltpu.VMEM(square, jnp.bfloat16),
            pltpu.SemaphoreType.DMA((items,)),
            pltpu.SemaphoreType.DMA((items,)),
            pltpu.SemaphoreType.DMA((items,)),
            pltpu.SemaphoreType.DMA((items,)),
            pltpu.SemaphoreType.DMA((3, 2, items)),
            pltpu.SemaphoreType.DMA((3, 2, items)),
            pltpu.SemaphoreType.DMA((2,)),
        ],
        compiler_params=pltpu.CompilerParams(
            collective_id=0, has_side_effects=True, vmem_limit_bytes=VMEM_LIMIT),
        name="halo",
    )(table, table, geometry, panel)

    depth = 4
    return pl.pallas_call(
        functools.partial(product_kernel, nx, ny),
        out_shape=jax.ShapeDtypeStruct((fil, width), jnp.float32),
        in_specs=[smem, smem, vmem, anywhere, anywhere, anywhere, anywhere],
        out_specs=vmem,
        scratch_shapes=[
            pltpu.SMEM((blocks * near + 8,), jnp.int32),
            pltpu.SMEM((blocks * near + 8,), jnp.int32),
            pltpu.SMEM((blocks * near + 8,), jnp.int32),
            pltpu.VMEM((blocks, BLOCK, 32), jnp.bfloat16),
            pltpu.VMEM((blocks, BLOCK, 16), jnp.bfloat16),
            pltpu.VMEM((blocks, BLOCK, 80), jnp.bfloat16),
            pltpu.VMEM((near, 128, BLOCK), jnp.bfloat16),
            pltpu.VMEM((near, BLOCK, width), jnp.bfloat16),
            pltpu.VMEM(square, jnp.float32),
            pltpu.VMEM(square, jnp.float32),
            pltpu.VMEM(square, jnp.float32),
            pltpu.VMEM(square, jnp.float32),
            pltpu.VMEM(square, jnp.bfloat16),
            pltpu.VMEM(square, jnp.bfloat16),
            pltpu.VMEM((depth,) + square, jnp.bfloat16),
            pltpu.SemaphoreType.DMA((9, blocks)),
            pltpu.SemaphoreType.DMA((depth,)),
            pltpu.SemaphoreType.DMA,
        ],
        compiler_params=pltpu.CompilerParams(vmem_limit_bytes=VMEM_LIMIT),
        name="products",
    )(table, lists, geometry, feats, panel, pans, tiles)


def solution(mesh):
    nx, ny = mesh.shape["gx"], mesh.shape["gy"]
    in_specs = (
        P(None, ("gx", "gy")),
        P(("gx", "gy"), None),
        P(("gx", "gy")),
        P(("gx", "gy")),
        P(("gx", "gy")),
    )
    out_specs = P(("gx", "gy"), None)
    return jax.shard_map(functools.partial(shards, nx, ny), mesh=mesh, in_specs=in_specs,
                         out_specs=out_specs, check_vma=False)
```

```python
import functools

import jax
import jax.numpy as jnp
from jax import lax
from jax.experimental import pallas as pl
from jax.experimental.pallas import tpu as pltpu
from jax.sharding import PartitionSpec as P

BLOCK = 512
CHUNKS = 4
PART = 256
GRID = 16.0
MESH = pl.DeviceIdType.MESH
VMEM_LIMIT = 56 * 1024 * 1024


def split(value):
    high = value.astype(jnp.bfloat16).astype(jnp.float32)
    return high, value - high


def features(geo, gx, gy, own):
    kind = lax.broadcasted_iota(jnp.int32, geo.shape, 0)
    place = kind < 3
    centre = jnp.where(kind == 0, gx.astype(jnp.float32) + 0.5, jnp.where(kind == 1, gy.astype(jnp.float32) + 0.5, 4.0))
    local = geo - centre
    coarse = jnp.where(place, jnp.floor(local * GRID + 0.5) * (1.0 / GRID), 0.0)
    fine = jnp.where(place, local - coarse, 0.0)
    radius = jnp.where(kind == 7, geo, 0.0)
    fine_high, rest = split(fine)
    fine_mid, fine_low = split(rest)
    both_high, both_low = split(fine + radius)
    norm = jnp.broadcast_to(jnp.sum(coarse * coarse, axis=0, keepdims=True), geo.shape)
    extra = jnp.broadcast_to(jnp.sum((2.0 * coarse + fine) * fine + radius * radius, axis=0, keepdims=True), geo.shape)
    norm_high, norm_low = split(norm)
    extra_high, rest = split(extra)
    extra_mid, extra_low = split(rest)
    direction = jnp.where((kind >= 3) & (kind <= 5), geo * geo[6:7, :], 0.0)
    blank = jnp.zeros_like(geo)
    if own:
        high, low = split(direction * BLOCK ** (-0.5))
        norms = jnp.where(kind == 0, norm_high, jnp.where(kind == 1, norm_low, jnp.where(kind <= 3, 1.0, 0.0)))
        extras = jnp.where(kind == 0, extra_high, jnp.where(kind == 1, extra_mid, jnp.where(
            kind == 2, extra_low, jnp.where(kind <= 5, 1.0, 0.0))))
        groups = [high, high, low, blank, coarse, norms, both_high, both_high, both_low,
                  coarse, coarse, coarse, fine_high, fine_mid, fine_low, extras]
    else:
        high, low = split(direction)
        sign = jnp.where(place, -8.0, 8.0)
        norms = 4.0 * jnp.where(kind <= 1, 1.0, jnp.where(kind == 2, norm_high, jnp.where(kind == 3, norm_low, 0.0)))
        extras = 4.0 * jnp.where(kind <= 2, 1.0, jnp.where(kind == 3, extra_high, jnp.where(
            kind == 4, extra_mid, jnp.where(kind == 5, extra_low, 0.0))))
        double = -8.0 * coarse
        groups = [high, low, high, blank, double, norms, sign * both_high, sign * both_low, sign * both_high,
                  -8.0 * fine_high, -8.0 * fine_mid, -8.0 * fine_low, double, double, double, extras]
    return jnp.concatenate(groups, axis=0)


def prepare_own(block, geo_ref, gx, gy, own_along, own_coarse, own_fine):
    lanes = pl.ds(pl.multiple_of(block * BLOCK, BLOCK), BLOCK)
    turned = features(geo_ref[:, lanes], gx, gy, True).T.astype(jnp.bfloat16)
    own_along[block] = turned[:, 0:32]
    own_coarse[block] = turned[:, 32:48]
    own_fine[block] = turned[:, 48:128]


def align_part(c, a, b, own, feats, work):
    own_along, own_coarse, own_fine = own
    aligned, square = work
    here = pl.ds(c * PART, PART)
    aligned[here, :] = jnp.dot(own_along[a, here, :], feats[b, 0:32, :], preferred_element_type=jnp.float32)
    square[here, :] = jnp.dot(
        own_coarse[a, here, :], feats[b, 32:48, :], preferred_element_type=jnp.float32
    ) + jnp.dot(own_fine[a, here, :], feats[b, 48:128, :], preferred_element_type=jnp.float32)


def tile_part(c, work, tile):
    aligned, square = work
    for r in range(c * PART, (c + 1) * PART, 16):
        here = pl.ds(r, 16)
        four = square[here, :]
        guess = lax.rsqrt(four.astype(jnp.bfloat16)).astype(jnp.float32)
        root = 3.0 - (four * guess) * guess
        tile[here, :] = ((aligned[here, :] * guess) * root).astype(jnp.bfloat16)


def halo_kernel(nx, ny, table_ref, list_ref, geo_ref, pan_ref, lists, pans, tiles, feats,
                geos, own_along, own_coarse, own_fine, aligned0, aligned1, square0, square1, tile0, tile1,
                x_send, x_recv, z_send, z_recv, y_send, y_recv, out_sems):
    own = own_along, own_coarse, own_fine
    work0, work1 = (aligned0, square0), (aligned1, square1)
    gx = lax.axis_index("gx")
    gy = lax.axis_index("gy")
    fil = pan_ref.shape[0]
    step = fil // CHUNKS
    items = CHUNKS + 2
    blocks = fil // BLOCK
    pairs = tiles.shape[0] // 2
    odd = lax.rem(gx, 2)
    partner = gx + 1 - 2 * odd
    relay_to = gx + 2 - 4 * odd
    relay_from = gx - 2 + 4 * odd
    has_to = (relay_to >= 0) & (relay_to < nx)
    has_from = (relay_from >= 0) & (relay_from < nx)
    has_up = gy + 1 < ny
    has_down = gy >= 1
    near_row = 2 - 2 * odd
    far_row = 2 * odd

    def part(k, own, row, col):
        if k == 0:
            return list_ref if own else lists.at[row * 3 + col]
        if k == 1:
            return geo_ref if own else geos.at[row * 3 + col]
        rows = pl.ds((k - 2) * step, step)
        return pan_ref.at[rows] if own else pans.at[row * 3 + col, rows]

    def x_copy(k):
        return pltpu.make_async_remote_copy(
            src_ref=part(k, True, 1, 1), dst_ref=part(k, False, far_row, 1),
            send_sem=x_send.at[k], recv_sem=x_recv.at[k],
            device_id=(partner, gy), device_id_type=MESH)

    def x_arrival(k):
        return pltpu.make_async_remote_copy(
            src_ref=part(k, True, 1, 1), dst_ref=part(k, False, near_row, 1),
            send_sem=x_send.at[k], recv_sem=x_recv.at[k],
            device_id=(partner, gy), device_id_type=MESH)

    def z_copy(k):
        return pltpu.make_async_remote_copy(
            src_ref=part(k, False, near_row, 1), dst_ref=part(k, False, far_row, 1),
            send_sem=z_send.at[k], recv_sem=z_recv.at[k],
            device_id=(relay_to, gy), device_id_type=MESH)

    def y_copy(k, kind, up):
        row = (1, near_row, far_row)[kind]
        return pltpu.make_async_remote_copy(
            src_ref=part(k, kind == 0, row, 1), dst_ref=part(k, False, row, 0 if up else 2),
            send_sem=y_send.at[kind, 1 if up else 0, k], recv_sem=y_recv.at[kind, 1 if up else 0, k],
            device_id=(gx, gy + 1 if up else gy - 1), device_id_type=MESH)

    def y_arrival(k, kind, up):
        row = (1, near_row, far_row)[kind]
        return pltpu.make_async_remote_copy(
            src_ref=part(k, kind == 0, row, 1), dst_ref=part(k, False, row, 0 if up else 2),
            send_sem=y_send.at[kind, 1 if up else 0, k], recv_sem=y_recv.at[kind, 1 if up else 0, k],
            device_id=(gx, gy - 1 if up else gy + 1), device_id_type=MESH)

    barrier = pltpu.get_barrier_semaphore()

    def greet(target, there):
        @pl.when(there)
        def _():
            pl.semaphore_signal(barrier, inc=1, device_id=target, device_id_type=MESH)

    pl.semaphore_signal(barrier, inc=1, device_id=(partner, gy), device_id_type=MESH)
    greet((relay_to, gy), has_to)
    greet((relay_from, gy), has_from)
    greet((gx, gy + 1), has_up)
    greet((gx, gy - 1), has_down)
    total = 1
    for there in (has_to, has_from, has_up, has_down):
        total = total + jnp.where(there, 1, 0)
    pl.semaphore_wait(barrier, total)

    def y_starts(k, kind):
        @pl.when(has_up)
        def _():
            y_copy(k, kind, True).start()

        @pl.when(has_down)
        def _():
            y_copy(k, kind, False).start()

    for k in range(2):
        x_copy(k).start()
        y_starts(k, 0)
    for k in range(2, items):
        x_copy(k).start()
    y_starts(2, 0)

    def relay(k):
        x_arrival(k).wait_recv()

        @pl.when(has_to)
        def _():
            z_copy(k).start()

        y_starts(k, 1)

    def spread(k):
        @pl.when(has_from)
        def _():
            z_copy(k).wait_recv()
            y_starts(k, 2)

    def own_block(block, _):
        prepare_own(block, geo_ref, gx, gy, *own)
        lanes = pl.ds(pl.multiple_of(block * BLOCK, BLOCK), BLOCK)
        feats[4 * blocks + block] = features(geo_ref[:, lanes], gx, gy, False).astype(jnp.bfloat16)
        return 0

    lax.fori_loop(0, blocks, own_block, 0)
    for k in range(2):
        relay(k)
    for k in range(2):
        spread(k)
    for k in range(3, items):
        y_starts(k, 0)

    def near_blocks(slot):
        def near_block(block, _):
            lanes = pl.ds(pl.multiple_of(block * BLOCK, BLOCK), BLOCK)
            feats[slot * blocks + block] = features(geos[slot, :, lanes], gx, gy, False).astype(jnp.bfloat16)
            return 0

        lax.fori_loop(0, blocks, near_block, 0)

    near_blocks(near_row * 3 + 1)

    @pl.when(has_from)
    def _():
        near_blocks(far_row * 3 + 1)

    def y_gets(kind, up):
        gets = has_down if up else has_up
        return gets & has_from if kind == 2 else gets

    for kind in range(3):
        for up in (True, False):
            @pl.when(y_gets(kind, up))
            def _():
                y_arrival(1, kind, up).wait_recv()
                near_blocks((1, near_row, far_row)[kind] * 3 + (0 if up else 2))

    def slot_ids(s):
        return list_ref[0, s], list_ref[1, s]

    def out_copy(which, tile, s):
        return pltpu.make_async_copy(tile, tiles.at[s], out_sems.at[which])

    a0, b0 = slot_ids(0)
    for c in range(BLOCK // PART):
        align_part(c, a0, b0, own, feats, work0)

    events = {}
    for c, at in enumerate((1, 6, 11, 17)):
        events.setdefault(at * pairs // 32, []).append((relay, c + 2))
    for c, at in enumerate((6, 11, 17, 23)):
        events.setdefault(at * pairs // 32, []).append((spread, c + 2))

    def pair_step(i, _):
        for at, calls in events.items():
            @pl.when(i == at)
            def _():
                for call, k in calls:
                    call(k)

        for half, now, later, tile in ((0, work0, work1, tile0), (1, work1, work0, tile1)):
            s = 2 * i + half
            a_next, b_next = slot_ids(jnp.minimum(s + 1, 2 * pairs - 1))

            @pl.when(i > 0)
            def _():
                out_copy(half, tile, s).wait()

            for c in range(BLOCK // PART):
                align_part(c, a_next, b_next, own, feats, later)
                tile_part(c, now, tile)
            out_copy(half, tile, s).start()
        return 0

    lax.fori_loop(0, pairs, pair_step, 0)
    out_copy(0, tile0, 2 * pairs - 2).wait()
    out_copy(1, tile1, 2 * pairs - 1).wait()

    for k in range(items):
        x_copy(k).wait_send()

        @pl.when(has_to)
        def _():
            z_copy(k).wait_send()

        for kind in range(3):
            for up, sends, gets in ((True, has_up, has_down), (False, has_down, has_up)):
                if kind == 2:
                    sends = sends & has_from
                    gets = gets & has_from

                @pl.when(sends)
                def _():
                    y_copy(k, kind, up).wait_send()

                if k != 1:
                    @pl.when(gets)
                    def _():
                        y_arrival(k, kind, up).wait_recv()


def product_kernel(nx, ny, list_ref, lists, geo_ref, feats_ref, pan_ref, pans, tiles,
                   out_ref, count_of, todo, slot_of, own_along, own_coarse, own_fine, feats, pan_all,
                   aligned0, aligned1, square0, square1, tile0, tile1, stored, sems, stored_sems, feat_sem):
    own = own_along, own_coarse, own_fine
    work0, work1 = (aligned0, square0), (aligned1, square1)
    gx = lax.axis_index("gx")
    gy = lax.axis_index("gy")
    fil, width = pan_ref.shape
    blocks = fil // BLOCK
    near = 9 * blocks
    spare = blocks * near
    sides = [(sx, sy) for sx in range(3) for sy in range(3)]

    def present(slot):
        sx, sy = sides[slot]
        there = (gx + (sx - 1) >= 0) & (gx + (sx - 1) < nx)
        return there & (gy + (sy - 1) >= 0) & (gy + (sy - 1) < ny)

    def load(slot, block):
        source = pan_ref.at[pl.ds(block * BLOCK, BLOCK)] if slot == 4 else pans.at[slot, pl.ds(block * BLOCK, BLOCK)]
        return pltpu.make_async_copy(source, pan_all.at[slot * blocks + block], sems.at[slot, block])

    feat_load = pltpu.make_async_copy(feats_ref, feats, feat_sem)
    for slot in (4, 0, 1, 2, 3, 5, 6, 7, 8):
        for block in range(blocks):
            load(slot, block).start()
    feat_load.start()

    def clear(i, _):
        count_of[i] = 0
        return 0

    lax.fori_loop(0, spare + 8, clear, 0, unroll=8)

    def add(a, b, wanted, n):
        where_ = jnp.where(wanted, a * near + b, spare)
        seen = count_of[where_]
        todo[n] = where_
        count_of[where_] = seen + 1
        return n + jnp.where(wanted & (seen == 0), 1, 0)

    def own_pair(s, n):
        slot_of[n] = s
        return add(list_ref[0, s], list_ref[1, s], True, n)

    ready = lax.fori_loop(0, list_ref[2, 0], own_pair, 0)
    depth = stored.shape[0]

    def fetch(i):
        slot = lax.rem(i, depth)
        return pltpu.make_async_copy(tiles.at[slot_of[i]], stored.at[slot], stored_sems.at[slot])

    for i in range(depth):
        @pl.when(i < ready)
        def _():
            fetch(i).start()

    def mirrored(s, n):
        q = list_ref[1, s] - 4 * blocks
        a = list_ref[0, s]
        return add(q, 4 * blocks + a, (q >= 0) & (q < blocks) & (q != a), n)

    n = lax.fori_loop(0, list_ref[2, 0], mirrored, ready)
    for slot in range(9):
        if slot != 4:
            def their_pair(s, n, slot=slot):
                q = lists[slot, 1, s] - (8 - slot) * blocks
                return add(q, slot * blocks + lists[slot, 0, s], (q >= 0) & (q < blocks), n)

            total = jnp.where(present(slot), lists[slot, 2, 0], 0)
            n = lax.fori_loop(0, total, their_pair, n)

    def own_block(block, _):
        prepare_own(block, geo_ref, gx, gy, *own)
        return 0

    lax.fori_loop(0, blocks, own_block, 0)
    out_ref[...] = jnp.zeros_like(out_ref)
    for slot in range(9):
        for block in range(blocks):
            load(slot, block).wait()

    def entry(i):
        inside = i < n
        index = jnp.where(inside, todo[jnp.where(inside, i, 0)], 4 * blocks)
        a = index // near
        return a, index - a * near, jnp.where(inside, count_of[index], 0).astype(jnp.float32)

    def product_part(c, a, b, times, tile):
        first = pl.multiple_of(a * BLOCK + c * PART, PART)
        product = jnp.dot(tile[pl.ds(c * PART, PART), :], pan_all[b], preferred_element_type=jnp.float32)
        out_ref[pl.ds(first, PART), :] += times * product

    def ready_item(i, _):
        a, b, times = entry(i)
        fetch(i).wait()
        for c in range(BLOCK // PART):
            product_part(c, a, b, times, stored.at[lax.rem(i, depth)])

        @pl.when(i + depth < ready)
        def _():
            fetch(i + depth).start()

        return 0

    lax.fori_loop(0, ready, ready_item, 0)
    feat_load.wait()

    @pl.when(n > ready)
    def _():
        a0, b0, _ = entry(ready)
        for c in range(BLOCK // PART):
            align_part(c, a0, b0, own, feats, work0)
        tile1[...] = jnp.zeros_like(tile1)

        def two_items(j, before):
            i = ready + 2 * j
            for half, now, later, tile, past in (
                (0, work0, work1, tile0, tile1), (1, work1, work0, tile1, tile0)):
                a, b, times = entry(i + half)
                a_next, b_next, _ = entry(i + half + 1)
                for c in range(BLOCK // PART):
                    align_part(c, a_next, b_next, own, feats, later)
                    tile_part(c, now, tile)
                    product_part(c, *before, past)
                before = (a, b, times)
            return before

        last = lax.fori_loop(0, (n - ready + 1) // 2, two_items, (jnp.int32(0), jnp.int32(4 * blocks), jnp.float32(0)))
        for c in range(BLOCK // PART):
            product_part(c, *last, tile1)


def shards(nx, ny, geometry, panel, pair_first, pair_second, pair_count):
    fil, width = panel.shape
    blocks = fil // BLOCK
    near = 9 * blocks
    pair_len = pair_first.shape[0]
    long = -(-pair_len // 128) * 128
    made = 2 * (-(-pair_len // 2))
    table = jnp.pad(jnp.stack([pair_first, pair_second, jnp.broadcast_to(pair_count, (pair_len,))]),
                    ((0, 5), (0, long - pair_len)))
    items = CHUNKS + 2
    anywhere = pl.BlockSpec(memory_space=pl.ANY)
    vmem = pl.BlockSpec(memory_space=pltpu.VMEM)
    smem = pl.BlockSpec(memory_space=pltpu.SMEM)
    square = (BLOCK, BLOCK)
    lists, pans, tiles, feats = pl.pallas_call(
        functools.partial(halo_kernel, nx, ny),
        out_shape=(
            jax.ShapeDtypeStruct((9, 8, long), jnp.int32),
            jax.ShapeDtypeStruct((9, fil, width), jnp.bfloat16),
            jax.ShapeDtypeStruct((made,) + square, jnp.bfloat16),
            jax.ShapeDtypeStruct((near, 128, BLOCK), jnp.bfloat16),
        ),
        in_specs=[anywhere, smem, vmem, anywhere],
        out_specs=(anywhere, anywhere, anywhere, vmem),
        scratch_shapes=[
            pltpu.VMEM((9, 8, fil), jnp.float32),
            pltpu.VMEM((blocks, BLOCK, 32), jnp.bfloat16),
            pltpu.VMEM((blocks, BLOCK, 16), jnp.bfloat16),
            pltpu.VMEM((blocks, BLOCK, 80), jnp.bfloat16),
            pltpu.VMEM(square, jnp.float32),
            pltpu.VMEM(square, jnp.float32),
            pltpu.VMEM(square, jnp.float32),
            pltpu.VMEM(square, jnp.float32),
            pltpu.VMEM(square, jnp.bfloat16),
            pltpu.VMEM(square, jnp.bfloat16),
            pltpu.SemaphoreType.DMA((items,)),
            pltpu.SemaphoreType.DMA((items,)),
            pltpu.SemaphoreType.DMA((items,)),
            pltpu.SemaphoreType.DMA((items,)),
            pltpu.SemaphoreType.DMA((3, 2, items)),
            pltpu.SemaphoreType.DMA((3, 2, items)),
            pltpu.SemaphoreType.DMA((2,)),
        ],
        compiler_params=pltpu.CompilerParams(
            collective_id=0, has_side_effects=True, vmem_limit_bytes=VMEM_LIMIT),
        name="halo",
    )(table, table, geometry, panel)

    depth = 4
    return pl.pallas_call(
        functools.partial(product_kernel, nx, ny),
        out_shape=jax.ShapeDtypeStruct((fil, width), jnp.float32),
        in_specs=[smem, smem, vmem, anywhere, anywhere, anywhere, anywhere],
        out_specs=vmem,
        scratch_shapes=[
            pltpu.SMEM((blocks * near + 8,), jnp.int32),
            pltpu.SMEM((blocks * near + 8,), jnp.int32),
            pltpu.SMEM((blocks * near + 8,), jnp.int32),
            pltpu.VMEM((blocks, BLOCK, 32), jnp.bfloat16),
            pltpu.VMEM((blocks, BLOCK, 16), jnp.bfloat16),
            pltpu.VMEM((blocks, BLOCK, 80), jnp.bfloat16),
            pltpu.VMEM((near, 128, BLOCK), jnp.bfloat16),
            pltpu.VMEM((near, BLOCK, width), jnp.bfloat16),
            pltpu.VMEM(square, jnp.float32),
            pltpu.VMEM(square, jnp.float32),
            pltpu.VMEM(square, jnp.float32),
            pltpu.VMEM(square, jnp.float32),
            pltpu.VMEM(square, jnp.bfloat16),
            pltpu.VMEM(square, jnp.bfloat16),
            pltpu.VMEM((depth,) + square, jnp.bfloat16),
            pltpu.SemaphoreType.DMA((9, blocks)),
            pltpu.SemaphoreType.DMA((depth,)),
            pltpu.SemaphoreType.DMA,
        ],
        compiler_params=pltpu.CompilerParams(vmem_limit_bytes=VMEM_LIMIT),
        name="products",
    )(table, lists, geometry, feats, panel, pans, tiles)


def solution(mesh):
    nx, ny = mesh.shape["gx"], mesh.shape["gy"]
    in_specs = (
        P(None, ("gx", "gy")),
        P(("gx", "gy"), None),
        P(("gx", "gy")),
        P(("gx", "gy")),
        P(("gx", "gy")),
    )
    out_specs = P(("gx", "gy"), None)
    return jax.shard_map(functools.partial(shards, nx, ny), mesh=mesh, in_specs=in_specs,
                         out_specs=out_specs, check_vma=False)
```

```python
import functools

import jax
import jax.numpy as jnp
from jax import lax
from jax.experimental import pallas as pl
from jax.experimental.pallas import tpu as pltpu
from jax.sharding import PartitionSpec as P

BLOCK = 512
CHUNKS = 4
PART = 512
GRID = 16.0
MESH = pl.DeviceIdType.MESH
VMEM_LIMIT = 56 * 1024 * 1024


def split(value):
    high = value.astype(jnp.bfloat16).astype(jnp.float32)
    return high, value - high


def features(geo, gx, gy, own):
    kind = lax.broadcasted_iota(jnp.int32, geo.shape, 0)
    place = kind < 3
    centre = jnp.where(kind == 0, gx.astype(jnp.float32) + 0.5, jnp.where(kind == 1, gy.astype(jnp.float32) + 0.5, 4.0))
    local = geo - centre
    coarse = jnp.where(place, jnp.floor(local * GRID + 0.5) * (1.0 / GRID), 0.0)
    fine = jnp.where(place, local - coarse, 0.0)
    radius = jnp.where(kind == 7, geo, 0.0)
    fine_high, rest = split(fine)
    fine_mid, fine_low = split(rest)
    both_high, both_low = split(fine + radius)
    norm = jnp.broadcast_to(jnp.sum(coarse * coarse, axis=0, keepdims=True), geo.shape)
    extra = jnp.broadcast_to(jnp.sum((2.0 * coarse + fine) * fine + radius * radius, axis=0, keepdims=True), geo.shape)
    norm_high, norm_low = split(norm)
    extra_high, rest = split(extra)
    extra_mid, extra_low = split(rest)
    direction = jnp.where((kind >= 3) & (kind <= 5), geo * geo[6:7, :], 0.0)
    blank = jnp.zeros_like(geo)
    if own:
        high, low = split(direction * BLOCK ** (-0.5))
        norms = jnp.where(kind == 0, norm_high, jnp.where(kind == 1, norm_low, jnp.where(kind <= 3, 1.0, 0.0)))
        extras = jnp.where(kind == 0, extra_high, jnp.where(kind == 1, extra_mid, jnp.where(
            kind == 2, extra_low, jnp.where(kind <= 5, 1.0, 0.0))))
        groups = [high, high, low, blank, coarse, norms, both_high, both_high, both_low,
                  coarse, coarse, coarse, fine_high, fine_mid, fine_low, extras]
    else:
        high, low = split(direction)
        sign = jnp.where(place, -2.0, 2.0)
        norms = jnp.where(kind <= 1, 1.0, jnp.where(kind == 2, norm_high, jnp.where(kind == 3, norm_low, 0.0)))
        extras = jnp.where(kind <= 2, 1.0, jnp.where(kind == 3, extra_high, jnp.where(
            kind == 4, extra_mid, jnp.where(kind == 5, extra_low, 0.0))))
        double = -2.0 * coarse
        groups = [high, low, high, blank, double, norms, sign * both_high, sign * both_low, sign * both_high,
                  -2.0 * fine_high, -2.0 * fine_mid, -2.0 * fine_low, double, double, double, extras]
    return jnp.concatenate(groups, axis=0)


def prepare_own(block, geo_ref, gx, gy, own_along, own_coarse, own_fine):
    lanes = pl.ds(pl.multiple_of(block * BLOCK, BLOCK), BLOCK)
    turned = features(geo_ref[:, lanes], gx, gy, True).T.astype(jnp.bfloat16)
    own_along[block] = turned[:, 0:32]
    own_coarse[block] = turned[:, 32:48]
    own_fine[block] = turned[:, 48:128]


def align_part(c, a, b, own, feats, work):
    own_along, own_coarse, own_fine = own
    aligned, square = work
    here = pl.ds(c * PART, PART)
    aligned[here, :] = jnp.dot(own_along[a, here, :], feats[b, 0:32, :], preferred_element_type=jnp.float32)
    square[here, :] = jnp.dot(
        own_coarse[a, here, :], feats[b, 32:48, :], preferred_element_type=jnp.float32
    ) + jnp.dot(own_fine[a, here, :], feats[b, 48:128, :], preferred_element_type=jnp.float32)


def tile_part(c, work, tile):
    aligned, square = work
    for r in range(c * PART, (c + 1) * PART, 16):
        here = pl.ds(r, 16)
        tile[here, :] = (aligned[here, :] * lax.rsqrt(square[here, :])).astype(jnp.bfloat16)


def halo_kernel(nx, ny, table_ref, list_ref, geo_ref, pan_ref, lists, pans, tiles, feats,
                geos, own_along, own_coarse, own_fine, aligned0, aligned1, square0, square1, tile0, tile1,
                x_send, x_recv, z_send, z_recv, y_send, y_recv, out_sems):
    own = own_along, own_coarse, own_fine
    work0, work1 = (aligned0, square0), (aligned1, square1)
    gx = lax.axis_index("gx")
    gy = lax.axis_index("gy")
    fil = pan_ref.shape[0]
    step = fil // CHUNKS
    items = CHUNKS + 2
    blocks = fil // BLOCK
    pairs = tiles.shape[0] // 2
    odd = lax.rem(gx, 2)
    partner = gx + 1 - 2 * odd
    relay_to = gx + 2 - 4 * odd
    relay_from = gx - 2 + 4 * odd
    has_to = (relay_to >= 0) & (relay_to < nx)
    has_from = (relay_from >= 0) & (relay_from < nx)
    has_up = gy + 1 < ny
    has_down = gy >= 1
    near_row = 2 - 2 * odd
    far_row = 2 * odd

    def part(k, own, row, col):
        if k == 0:
            return list_ref if own else lists.at[row * 3 + col]
        if k == 1:
            return geo_ref if own else geos.at[row * 3 + col]
        rows = pl.ds((k - 2) * step, step)
        return pan_ref.at[rows] if own else pans.at[row * 3 + col, rows]

    def x_copy(k):
        return pltpu.make_async_remote_copy(
            src_ref=part(k, True, 1, 1), dst_ref=part(k, False, far_row, 1),
            send_sem=x_send.at[k], recv_sem=x_recv.at[k],
            device_id=(partner, gy), device_id_type=MESH)

    def x_arrival(k):
        return pltpu.make_async_remote_copy(
            src_ref=part(k, True, 1, 1), dst_ref=part(k, False, near_row, 1),
            send_sem=x_send.at[k], recv_sem=x_recv.at[k],
            device_id=(partner, gy), device_id_type=MESH)

    def z_copy(k):
        return pltpu.make_async_remote_copy(
            src_ref=part(k, False, near_row, 1), dst_ref=part(k, False, far_row, 1),
            send_sem=z_send.at[k], recv_sem=z_recv.at[k],
            device_id=(relay_to, gy), device_id_type=MESH)

    def y_copy(k, kind, up):
        row = (1, near_row, far_row)[kind]
        return pltpu.make_async_remote_copy(
            src_ref=part(k, kind == 0, row, 1), dst_ref=part(k, False, row, 0 if up else 2),
            send_sem=y_send.at[kind, 1 if up else 0, k], recv_sem=y_recv.at[kind, 1 if up else 0, k],
            device_id=(gx, gy + 1 if up else gy - 1), device_id_type=MESH)

    def y_arrival(k, kind, up):
        row = (1, near_row, far_row)[kind]
        return pltpu.make_async_remote_copy(
            src_ref=part(k, kind == 0, row, 1), dst_ref=part(k, False, row, 0 if up else 2),
            send_sem=y_send.at[kind, 1 if up else 0, k], recv_sem=y_recv.at[kind, 1 if up else 0, k],
            device_id=(gx, gy - 1 if up else gy + 1), device_id_type=MESH)

    barrier = pltpu.get_barrier_semaphore()

    def greet(target, there):
        @pl.when(there)
        def _():
            pl.semaphore_signal(barrier, inc=1, device_id=target, device_id_type=MESH)

    pl.semaphore_signal(barrier, inc=1, device_id=(partner, gy), device_id_type=MESH)
    greet((relay_to, gy), has_to)
    greet((relay_from, gy), has_from)
    greet((gx, gy + 1), has_up)
    greet((gx, gy - 1), has_down)
    total = 1
    for there in (has_to, has_from, has_up, has_down):
        total = total + jnp.where(there, 1, 0)
    pl.semaphore_wait(barrier, total)

    def y_starts(k, kind):
        @pl.when(has_up)
        def _():
            y_copy(k, kind, True).start()

        @pl.when(has_down)
        def _():
            y_copy(k, kind, False).start()

    for k in range(2):
        x_copy(k).start()
        y_starts(k, 0)
    for k in range(2, items):
        x_copy(k).start()
    y_starts(2, 0)

    def relay(k):
        x_arrival(k).wait_recv()

        @pl.when(has_to)
        def _():
            z_copy(k).start()

        y_starts(k, 1)

    def spread(k):
        @pl.when(has_from)
        def _():
            z_copy(k).wait_recv()
            y_starts(k, 2)

    def own_block(block, _):
        prepare_own(block, geo_ref, gx, gy, *own)
        lanes = pl.ds(pl.multiple_of(block * BLOCK, BLOCK), BLOCK)
        feats[4 * blocks + block] = features(geo_ref[:, lanes], gx, gy, False).astype(jnp.bfloat16)
        return 0

    lax.fori_loop(0, blocks, own_block, 0)
    for k in range(2):
        relay(k)
    for k in range(2):
        spread(k)
    for k in range(3, items):
        y_starts(k, 0)

    def near_blocks(slot):
        def near_block(block, _):
            lanes = pl.ds(pl.multiple_of(block * BLOCK, BLOCK), BLOCK)
            feats[slot * blocks + block] = features(geos[slot, :, lanes], gx, gy, False).astype(jnp.bfloat16)
            return 0

        lax.fori_loop(0, blocks, near_block, 0)

    near_blocks(near_row * 3 + 1)

    @pl.when(has_from)
    def _():
        near_blocks(far_row * 3 + 1)

    def y_gets(kind, up):
        gets = has_down if up else has_up
        return gets & has_from if kind == 2 else gets

    for kind in range(3):
        for up in (True, False):
            @pl.when(y_gets(kind, up))
            def _():
                y_arrival(1, kind, up).wait_recv()
                near_blocks((1, near_row, far_row)[kind] * 3 + (0 if up else 2))

    def slot_ids(s):
        return list_ref[0, s], list_ref[1, s]

    def out_copy(which, tile, s):
        return pltpu.make_async_copy(tile, tiles.at[s], out_sems.at[which])

    a0, b0 = slot_ids(0)
    for c in range(BLOCK // PART):
        align_part(c, a0, b0, own, feats, work0)

    events = {}
    for c, at in enumerate((1, 6, 11, 17)):
        events.setdefault(at * pairs // 32, []).append((relay, c + 2))
    for c, at in enumerate((6, 11, 17, 23)):
        events.setdefault(at * pairs // 32, []).append((spread, c + 2))

    def pair_step(i, _):
        for at, calls in events.items():
            @pl.when(i == at)
            def _():
                for call, k in calls:
                    call(k)

        for half, now, later, tile in ((0, work0, work1, tile0), (1, work1, work0, tile1)):
            s = 2 * i + half
            a_next, b_next = slot_ids(jnp.minimum(s + 1, 2 * pairs - 1))

            @pl.when(i > 0)
            def _():
                out_copy(half, tile, s).wait()

            for c in range(BLOCK // PART):
                align_part(c, a_next, b_next, own, feats, later)
                tile_part(c, now, tile)
            out_copy(half, tile, s).start()
        return 0

    lax.fori_loop(0, pairs, pair_step, 0)
    out_copy(0, tile0, 2 * pairs - 2).wait()
    out_copy(1, tile1, 2 * pairs - 1).wait()

    for k in range(items):
        x_copy(k).wait_send()

        @pl.when(has_to)
        def _():
            z_copy(k).wait_send()

        for kind in range(3):
            for up, sends, gets in ((True, has_up, has_down), (False, has_down, has_up)):
                if kind == 2:
                    sends = sends & has_from
                    gets = gets & has_from

                @pl.when(sends)
                def _():
                    y_copy(k, kind, up).wait_send()

                if k != 1:
                    @pl.when(gets)
                    def _():
                        y_arrival(k, kind, up).wait_recv()


def product_kernel(nx, ny, list_ref, lists, geo_ref, feats_ref, pan_ref, pans, tiles,
                   out_ref, count_of, todo, slot_of, own_along, own_coarse, own_fine, feats, pan_all,
                   aligned0, aligned1, square0, square1, tile0, tile1, product, stored, sems, stored_sems, feat_sem):
    own = own_along, own_coarse, own_fine
    work0, work1 = (aligned0, square0), (aligned1, square1)
    gx = lax.axis_index("gx")
    gy = lax.axis_index("gy")
    fil, width = pan_ref.shape
    blocks = fil // BLOCK
    near = 9 * blocks
    spare = blocks * near
    sides = [(sx, sy) for sx in range(3) for sy in range(3)]

    def present(slot):
        sx, sy = sides[slot]
        there = (gx + (sx - 1) >= 0) & (gx + (sx - 1) < nx)
        return there & (gy + (sy - 1) >= 0) & (gy + (sy - 1) < ny)

    def load(slot, block):
        source = pan_ref.at[pl.ds(block * BLOCK, BLOCK)] if slot == 4 else pans.at[slot, pl.ds(block * BLOCK, BLOCK)]
        return pltpu.make_async_copy(source, pan_all.at[slot * blocks + block], sems.at[slot, block])

    feat_load = pltpu.make_async_copy(feats_ref, feats, feat_sem)
    for slot in (4, 0, 1, 2, 3, 5, 6, 7, 8):
        for block in range(blocks):
            load(slot, block).start()
    feat_load.start()

    def clear(i, _):
        count_of[i] = 0
        return 0

    lax.fori_loop(0, spare + 8, clear, 0, unroll=8)

    def add(a, b, wanted, n):
        where_ = jnp.where(wanted, a * near + b, spare)
        seen = count_of[where_]
        todo[n] = where_
        count_of[where_] = seen + 1
        return n + jnp.where(wanted & (seen == 0), 1, 0)

    def own_pair(s, n):
        slot_of[n] = s
        return add(list_ref[0, s], list_ref[1, s], True, n)

    ready = lax.fori_loop(0, list_ref[2, 0], own_pair, 0)
    depth = stored.shape[0]

    def fetch(i):
        slot = lax.rem(i, depth)
        return pltpu.make_async_copy(tiles.at[slot_of[i]], stored.at[slot], stored_sems.at[slot])

    for i in range(depth):
        @pl.when(i < ready)
        def _():
            fetch(i).start()

    def mirrored(s, n):
        q = list_ref[1, s] - 4 * blocks
        a = list_ref[0, s]
        return add(q, 4 * blocks + a, (q >= 0) & (q < blocks) & (q != a), n)

    n = lax.fori_loop(0, list_ref[2, 0], mirrored, ready)
    for slot in range(9):
        if slot != 4:
            def their_pair(s, n, slot=slot):
                q = lists[slot, 1, s] - (8 - slot) * blocks
                return add(q, slot * blocks + lists[slot, 0, s], (q >= 0) & (q < blocks), n)

            total = jnp.where(present(slot), lists[slot, 2, 0], 0)
            n = lax.fori_loop(0, total, their_pair, n)

    def own_block(block, _):
        prepare_own(block, geo_ref, gx, gy, *own)
        return 0

    lax.fori_loop(0, blocks, own_block, 0)
    out_ref[...] = jnp.zeros_like(out_ref)
    for slot in range(9):
        for block in range(blocks):
            load(slot, block).wait()

    def entry(i):
        inside = i < n
        index = jnp.where(inside, todo[jnp.where(inside, i, 0)], 4 * blocks)
        a = index // near
        return a, index - a * near, jnp.where(inside, count_of[index], 0).astype(jnp.float32)

    def product_part(c, a, b, times, tile):
        first = pl.multiple_of(a * BLOCK + c * PART, PART)
        here = jnp.dot(tile[pl.ds(c * PART, PART), :], pan_all[b], preferred_element_type=jnp.float32)
        out_ref[pl.ds(first, PART), :] += times * here

    def ready_item(i, _):
        a, b, times = entry(i)
        fetch(i).wait()
        for c in range(BLOCK // PART):
            product_part(c, a, b, times, stored.at[lax.rem(i, depth)])

        @pl.when(i + depth < ready)
        def _():
            fetch(i + depth).start()

        return 0

    lax.fori_loop(0, ready, ready_item, 0)
    feat_load.wait()

    @pl.when(n > ready)
    def _():
        a0, b0, _ = entry(ready)
        for c in range(BLOCK // PART):
            align_part(c, a0, b0, own, feats, work0)
        tile1[...] = jnp.zeros_like(tile1)

        def two_items(j, before):
            i = ready + 2 * j
            for half, now, later, tile, past in (
                (0, work0, work1, tile0, tile1), (1, work1, work0, tile1, tile0)):
                a, b, times = entry(i + half)
                a_next, b_next, _ = entry(i + half + 1)
                for c in range(BLOCK // PART):
                    align_part(c, a_next, b_next, own, feats, later)
                sum_a, sum_b, sum_times = before
                product[...] = jnp.dot(past[...], pan_all[sum_b], preferred_element_type=jnp.float32)
                for c in range(BLOCK // PART):
                    tile_part(c, now, tile)
                out_ref[pl.ds(pl.multiple_of(sum_a * BLOCK, BLOCK), BLOCK), :] += sum_times * product[...]
                before = (a, b, times)
            return before

        last = lax.fori_loop(0, (n - ready + 1) // 2, two_items, (jnp.int32(0), jnp.int32(4 * blocks), jnp.float32(0)))
        for c in range(BLOCK // PART):
            product_part(c, *last, tile1)


def shards(nx, ny, geometry, panel, pair_first, pair_second, pair_count):
    fil, width = panel.shape
    blocks = fil // BLOCK
    near = 9 * blocks
    pair_len = pair_first.shape[0]
    long = -(-pair_len // 128) * 128
    made = 2 * (-(-pair_len // 2))
    table = jnp.pad(jnp.stack([pair_first, pair_second, jnp.broadcast_to(pair_count, (pair_len,))]),
                    ((0, 5), (0, long - pair_len)))
    items = CHUNKS + 2
    anywhere = pl.BlockSpec(memory_space=pl.ANY)
    vmem = pl.BlockSpec(memory_space=pltpu.VMEM)
    smem = pl.BlockSpec(memory_space=pltpu.SMEM)
    square = (BLOCK, BLOCK)
    lists, pans, tiles, feats = pl.pallas_call(
        functools.partial(halo_kernel, nx, ny),
        out_shape=(
            jax.ShapeDtypeStruct((9, 8, long), jnp.int32),
            jax.ShapeDtypeStruct((9, fil, width), jnp.bfloat16),
            jax.ShapeDtypeStruct((made,) + square, jnp.bfloat16),
            jax.ShapeDtypeStruct((near, 128, BLOCK), jnp.bfloat16),
        ),
        in_specs=[anywhere, smem, vmem, anywhere],
        out_specs=(anywhere, anywhere, anywhere, vmem),
        scratch_shapes=[
            pltpu.VMEM((9, 8, fil), jnp.float32),
            pltpu.VMEM((blocks, BLOCK, 32), jnp.bfloat16),
            pltpu.VMEM((blocks, BLOCK, 16), jnp.bfloat16),
            pltpu.VMEM((blocks, BLOCK, 80), jnp.bfloat16),
            pltpu.VMEM(square, jnp.float32),
            pltpu.VMEM(square, jnp.float32),
            pltpu.VMEM(square, jnp.float32),
            pltpu.VMEM(square, jnp.float32),
            pltpu.VMEM(square, jnp.bfloat16),
            pltpu.VMEM(square, jnp.bfloat16),
            pltpu.SemaphoreType.DMA((items,)),
            pltpu.SemaphoreType.DMA((items,)),
            pltpu.SemaphoreType.DMA((items,)),
            pltpu.SemaphoreType.DMA((items,)),
            pltpu.SemaphoreType.DMA((3, 2, items)),
            pltpu.SemaphoreType.DMA((3, 2, items)),
            pltpu.SemaphoreType.DMA((2,)),
        ],
        compiler_params=pltpu.CompilerParams(
            collective_id=0, has_side_effects=True, vmem_limit_bytes=VMEM_LIMIT),
        name="halo",
    )(table, table, geometry, panel)

    depth = 4
    return pl.pallas_call(
        functools.partial(product_kernel, nx, ny),
        out_shape=jax.ShapeDtypeStruct((fil, width), jnp.float32),
        in_specs=[smem, smem, vmem, anywhere, anywhere, anywhere, anywhere],
        out_specs=vmem,
        scratch_shapes=[
            pltpu.SMEM((blocks * near + 8,), jnp.int32),
            pltpu.SMEM((blocks * near + 8,), jnp.int32),
            pltpu.SMEM((blocks * near + 8,), jnp.int32),
            pltpu.VMEM((blocks, BLOCK, 32), jnp.bfloat16),
            pltpu.VMEM((blocks, BLOCK, 16), jnp.bfloat16),
            pltpu.VMEM((blocks, BLOCK, 80), jnp.bfloat16),
            pltpu.VMEM((near, 128, BLOCK), jnp.bfloat16),
            pltpu.VMEM((near, BLOCK, width), jnp.bfloat16),
            pltpu.VMEM(square, jnp.float32),
            pltpu.VMEM(square, jnp.float32),
            pltpu.VMEM(square, jnp.float32),
            pltpu.VMEM(square, jnp.float32),
            pltpu.VMEM(square, jnp.bfloat16),
            pltpu.VMEM(square, jnp.bfloat16),
            pltpu.VMEM((BLOCK, width), jnp.float32),
            pltpu.VMEM((depth,) + square, jnp.bfloat16),
            pltpu.SemaphoreType.DMA((9, blocks)),
            pltpu.SemaphoreType.DMA((depth,)),
            pltpu.SemaphoreType.DMA,
        ],
        compiler_params=pltpu.CompilerParams(vmem_limit_bytes=VMEM_LIMIT),
        name="products",
    )(table, lists, geometry, feats, panel, pans, tiles)


def solution(mesh):
    nx, ny = mesh.shape["gx"], mesh.shape["gy"]
    in_specs = (
        P(None, ("gx", "gy")),
        P(("gx", "gy"), None),
        P(("gx", "gy")),
        P(("gx", "gy")),
        P(("gx", "gy")),
    )
    out_specs = P(("gx", "gy"), None)
    return jax.shard_map(functools.partial(shards, nx, ny), mesh=mesh, in_specs=in_specs,
                         out_specs=out_specs, check_vma=False)
```

```python
import functools

import jax
import jax.numpy as jnp
from jax import lax
from jax.experimental import pallas as pl
from jax.experimental.pallas import tpu as pltpu
from jax.sharding import PartitionSpec as P

BLOCK = 512
CHUNKS = 4
PART = 512
GRID = 16.0
MESH = pl.DeviceIdType.MESH
VMEM_LIMIT = 56 * 1024 * 1024


def split(value):
    high = value.astype(jnp.bfloat16).astype(jnp.float32)
    return high, value - high


def features(geo, gx, gy, own):
    kind = lax.broadcasted_iota(jnp.int32, geo.shape, 0)
    place = kind < 3
    centre = jnp.where(kind == 0, gx.astype(jnp.float32) + 0.5, jnp.where(kind == 1, gy.astype(jnp.float32) + 0.5, 4.0))
    local = geo - centre
    coarse = jnp.where(place, jnp.floor(local * GRID + 0.5) * (1.0 / GRID), 0.0)
    fine = jnp.where(place, local - coarse, 0.0)
    radius = jnp.where(kind == 7, geo, 0.0)
    fine_high, rest = split(fine)
    fine_mid, fine_low = split(rest)
    both_high, both_low = split(fine + radius)
    norm = jnp.broadcast_to(jnp.sum(coarse * coarse, axis=0, keepdims=True), geo.shape)
    extra = jnp.broadcast_to(jnp.sum((2.0 * coarse + fine) * fine + radius * radius, axis=0, keepdims=True), geo.shape)
    norm_high, norm_low = split(norm)
    extra_high, rest = split(extra)
    extra_mid, extra_low = split(rest)
    direction = jnp.where((kind >= 3) & (kind <= 5), geo * geo[6:7, :], 0.0)
    blank = jnp.zeros_like(geo)
    if own:
        high, low = split(direction * BLOCK ** (-0.5))
        norms = jnp.where(kind == 0, norm_high, jnp.where(kind == 1, norm_low, jnp.where(kind <= 3, 1.0, 0.0)))
        extras = jnp.where(kind == 0, extra_high, jnp.where(kind == 1, extra_mid, jnp.where(
            kind == 2, extra_low, jnp.where(kind <= 5, 1.0, 0.0))))
        groups = [high, high, low, blank, coarse, norms, both_high, both_high, both_low,
                  coarse, coarse, coarse, fine_high, fine_mid, fine_low, extras]
    else:
        high, low = split(direction)
        sign = jnp.where(place, -2.0, 2.0)
        norms = jnp.where(kind <= 1, 1.0, jnp.where(kind == 2, norm_high, jnp.where(kind == 3, norm_low, 0.0)))
        extras = jnp.where(kind <= 2, 1.0, jnp.where(kind == 3, extra_high, jnp.where(
            kind == 4, extra_mid, jnp.where(kind == 5, extra_low, 0.0))))
        double = -2.0 * coarse
        groups = [high, low, high, blank, double, norms, sign * both_high, sign * both_low, sign * both_high,
                  -2.0 * fine_high, -2.0 * fine_mid, -2.0 * fine_low, double, double, double, extras]
    return jnp.concatenate(groups, axis=0)


def prepare_own(block, geo_ref, gx, gy, own_along, own_coarse, own_fine):
    lanes = pl.ds(pl.multiple_of(block * BLOCK, BLOCK), BLOCK)
    turned = features(geo_ref[:, lanes], gx, gy, True).T.astype(jnp.bfloat16)
    own_along[block] = turned[:, 0:32]
    own_coarse[block] = turned[:, 32:48]
    own_fine[block] = turned[:, 48:128]


def align_part(c, a, b, own, feats, work):
    own_along, own_coarse, own_fine = own
    aligned, square = work
    here = pl.ds(c * PART, PART)
    aligned[here, :] = jnp.dot(own_along[a, here, :], feats[b, 0:32, :], preferred_element_type=jnp.float32)
    square[here, :] = jnp.dot(
        own_coarse[a, here, :], feats[b, 32:48, :], preferred_element_type=jnp.float32
    ) + jnp.dot(own_fine[a, here, :], feats[b, 48:128, :], preferred_element_type=jnp.float32)


def tile_part(c, work, tile):
    aligned, square = work
    for r in range(c * PART, (c + 1) * PART, 16):
        here = pl.ds(r, 16)
        tile[here, :] = (aligned[here, :] * lax.rsqrt(square[here, :])).astype(jnp.bfloat16)


def halo_kernel(nx, ny, table_ref, list_ref, geo_ref, pan_ref, lists, pans, tiles, feats,
                geos, own_along, own_coarse, own_fine, aligned0, aligned1, square0, square1, tile0, tile1, tile2, tile3,
                x_send, x_recv, z_send, z_recv, y_send, y_recv, out_sems):
    own = own_along, own_coarse, own_fine
    work0, work1 = (aligned0, square0), (aligned1, square1)
    gx = lax.axis_index("gx")
    gy = lax.axis_index("gy")
    fil = pan_ref.shape[0]
    step = fil // CHUNKS
    items = CHUNKS + 2
    blocks = fil // BLOCK
    rounds = tiles.shape[0] // 4
    odd = lax.rem(gx, 2)
    partner = gx + 1 - 2 * odd
    relay_to = gx + 2 - 4 * odd
    relay_from = gx - 2 + 4 * odd
    has_to = (relay_to >= 0) & (relay_to < nx)
    has_from = (relay_from >= 0) & (relay_from < nx)
    has_up = gy + 1 < ny
    has_down = gy >= 1
    near_row = 2 - 2 * odd
    far_row = 2 * odd

    def part(k, own, row, col):
        if k == 0:
            return list_ref if own else lists.at[row * 3 + col]
        if k == 1:
            return geo_ref if own else geos.at[row * 3 + col]
        rows = pl.ds((k - 2) * step, step)
        return pan_ref.at[rows] if own else pans.at[row * 3 + col, rows]

    def x_copy(k):
        return pltpu.make_async_remote_copy(
            src_ref=part(k, True, 1, 1), dst_ref=part(k, False, far_row, 1),
            send_sem=x_send.at[k], recv_sem=x_recv.at[k],
            device_id=(partner, gy), device_id_type=MESH)

    def x_arrival(k):
        return pltpu.make_async_remote_copy(
            src_ref=part(k, True, 1, 1), dst_ref=part(k, False, near_row, 1),
            send_sem=x_send.at[k], recv_sem=x_recv.at[k],
            device_id=(partner, gy), device_id_type=MESH)

    def z_copy(k):
        return pltpu.make_async_remote_copy(
            src_ref=part(k, False, near_row, 1), dst_ref=part(k, False, far_row, 1),
            send_sem=z_send.at[k], recv_sem=z_recv.at[k],
            device_id=(relay_to, gy), device_id_type=MESH)

    def y_copy(k, kind, up):
        row = (1, near_row, far_row)[kind]
        return pltpu.make_async_remote_copy(
            src_ref=part(k, kind == 0, row, 1), dst_ref=part(k, False, row, 0 if up else 2),
            send_sem=y_send.at[kind, 1 if up else 0, k], recv_sem=y_recv.at[kind, 1 if up else 0, k],
            device_id=(gx, gy + 1 if up else gy - 1), device_id_type=MESH)

    def y_arrival(k, kind, up):
        row = (1, near_row, far_row)[kind]
        return pltpu.make_async_remote_copy(
            src_ref=part(k, kind == 0, row, 1), dst_ref=part(k, False, row, 0 if up else 2),
            send_sem=y_send.at[kind, 1 if up else 0, k], recv_sem=y_recv.at[kind, 1 if up else 0, k],
            device_id=(gx, gy - 1 if up else gy + 1), device_id_type=MESH)

    barrier = pltpu.get_barrier_semaphore()

    def greet(target, there):
        @pl.when(there)
        def _():
            pl.semaphore_signal(barrier, inc=1, device_id=target, device_id_type=MESH)

    pl.semaphore_signal(barrier, inc=1, device_id=(partner, gy), device_id_type=MESH)
    greet((relay_to, gy), has_to)
    greet((relay_from, gy), has_from)
    greet((gx, gy + 1), has_up)
    greet((gx, gy - 1), has_down)
    total = 1
    for there in (has_to, has_from, has_up, has_down):
        total = total + jnp.where(there, 1, 0)
    pl.semaphore_wait(barrier, total)

    def y_starts(k, kind):
        @pl.when(has_up)
        def _():
            y_copy(k, kind, True).start()

        @pl.when(has_down)
        def _():
            y_copy(k, kind, False).start()

    for k in range(2):
        x_copy(k).start()
        y_starts(k, 0)
    def relay(k):
        x_arrival(k).wait_recv()

        @pl.when(has_to)
        def _():
            z_copy(k).start()

        y_starts(k, 1)

    def spread(k):
        @pl.when(has_from)
        def _():
            z_copy(k).wait_recv()
            y_starts(k, 2)

    def own_block(block, _):
        prepare_own(block, geo_ref, gx, gy, *own)
        lanes = pl.ds(pl.multiple_of(block * BLOCK, BLOCK), BLOCK)
        feats[4 * blocks + block] = features(geo_ref[:, lanes], gx, gy, False).astype(jnp.bfloat16)
        return 0

    lax.fori_loop(0, blocks, own_block, 0)
    for k in range(2):
        relay(k)
    for k in range(2, items):
        x_copy(k).start()
    for k in range(2):
        spread(k)
    for k in range(2, items):
        y_starts(k, 0)

    def near_blocks(slot):
        def near_block(block, _):
            lanes = pl.ds(pl.multiple_of(block * BLOCK, BLOCK), BLOCK)
            feats[slot * blocks + block] = features(geos[slot, :, lanes], gx, gy, False).astype(jnp.bfloat16)
            return 0

        lax.fori_loop(0, blocks, near_block, 0)

    near_blocks(near_row * 3 + 1)

    @pl.when(has_from)
    def _():
        near_blocks(far_row * 3 + 1)

    def y_gets(kind, up):
        gets = has_down if up else has_up
        return gets & has_from if kind == 2 else gets

    for kind in range(3):
        for up in (True, False):
            @pl.when(y_gets(kind, up))
            def _():
                y_arrival(1, kind, up).wait_recv()
                near_blocks((1, near_row, far_row)[kind] * 3 + (0 if up else 2))

    def slot_ids(s):
        return list_ref[0, s], list_ref[1, s]

    piece = BLOCK // 4

    def out_copies(which, tile, s):
        return [pltpu.make_async_copy(tile.at[pl.ds(c * piece, piece)], tiles.at[s, pl.ds(c * piece, piece)],
                                      out_sems.at[which, c]) for c in range(4)]

    a0, b0 = slot_ids(0)
    for c in range(BLOCK // PART):
        align_part(c, a0, b0, own, feats, work0)

    events = {}
    for c, at in enumerate((0, 2, 4, 7)):
        events.setdefault(at * rounds // 16, []).append((relay, c + 2))
    for c, at in enumerate((2, 4, 7, 9)):
        events.setdefault(at * rounds // 16, []).append((spread, c + 2))
    held = tile0, tile1, tile2, tile3

    def round_step(i, _):
        for at, calls in events.items():
            @pl.when(i == at)
            def _():
                for call, k in calls:
                    call(k)

        for which, tile in enumerate(held):
            now, later = (work0, work1) if which % 2 == 0 else (work1, work0)
            s = 4 * i + which
            a_next, b_next = slot_ids(jnp.minimum(s + 1, 4 * rounds - 1))

            @pl.when(i > 0)
            def _():
                for copy in out_copies(which, tile, s):
                    copy.wait()

            align_part(0, a_next, b_next, own, feats, later)
            tile_part(0, now, tile)
            for copy in out_copies(which, tile, s):
                copy.start()
        return 0

    lax.fori_loop(0, rounds, round_step, 0)
    for which, tile in enumerate(held):
        for copy in out_copies(which, tile, 4 * rounds - 4 + which):
            copy.wait()

    for k in range(items):
        x_copy(k).wait_send()

        @pl.when(has_to)
        def _():
            z_copy(k).wait_send()

        for kind in range(3):
            for up, sends, gets in ((True, has_up, has_down), (False, has_down, has_up)):
                if kind == 2:
                    sends = sends & has_from
                    gets = gets & has_from

                @pl.when(sends)
                def _():
                    y_copy(k, kind, up).wait_send()

                if k != 1:
                    @pl.when(gets)
                    def _():
                        y_arrival(k, kind, up).wait_recv()


def product_kernel(nx, ny, list_ref, lists, geo_ref, feats_ref, pan_ref, pans, tiles,
                   out_ref, count_of, todo, slot_of, own_along, own_coarse, own_fine, feats, pan_all,
                   aligned0, aligned1, square0, square1, tile0, tile1, product, stored, sems, stored_sems, feat_sem):
    own = own_along, own_coarse, own_fine
    work0, work1 = (aligned0, square0), (aligned1, square1)
    gx = lax.axis_index("gx")
    gy = lax.axis_index("gy")
    fil, width = pan_ref.shape
    blocks = fil // BLOCK
    near = 9 * blocks
    spare = blocks * near
    sides = [(sx, sy) for sx in range(3) for sy in range(3)]

    def present(slot):
        sx, sy = sides[slot]
        there = (gx + (sx - 1) >= 0) & (gx + (sx - 1) < nx)
        return there & (gy + (sy - 1) >= 0) & (gy + (sy - 1) < ny)

    def load(slot, block):
        source = pan_ref.at[pl.ds(block * BLOCK, BLOCK)] if slot == 4 else pans.at[slot, pl.ds(block * BLOCK, BLOCK)]
        return pltpu.make_async_copy(source, pan_all.at[slot * blocks + block], sems.at[slot, block])

    feat_load = pltpu.make_async_copy(feats_ref, feats, feat_sem)
    for slot in (4, 0, 1, 2, 3, 5, 6, 7, 8):
        for block in range(blocks):
            load(slot, block).start()
    feat_load.start()

    def clear(i, _):
        count_of[i] = 0
        return 0

    lax.fori_loop(0, spare + 8, clear, 0, unroll=8)

    def add(a, b, wanted, n):
        where_ = jnp.where(wanted, a * near + b, spare)
        seen = count_of[where_]
        todo[n] = where_
        count_of[where_] = seen + 1
        return n + jnp.where(wanted & (seen == 0), 1, 0)

    def own_pair(s, n):
        slot_of[n] = s
        return add(list_ref[0, s], list_ref[1, s], True, n)

    ready = lax.fori_loop(0, list_ref[2, 0], own_pair, 0)
    depth = stored.shape[0]

    def fetch(i):
        slot = lax.rem(i, depth)
        return pltpu.make_async_copy(tiles.at[slot_of[i]], stored.at[slot], stored_sems.at[slot])

    for i in range(depth):
        @pl.when(i < ready)
        def _():
            fetch(i).start()

    def mirrored(s, n):
        q = list_ref[1, s] - 4 * blocks
        a = list_ref[0, s]
        return add(q, 4 * blocks + a, (q >= 0) & (q < blocks) & (q != a), n)

    n = lax.fori_loop(0, list_ref[2, 0], mirrored, ready)
    for slot in range(9):
        if slot != 4:
            def their_pair(s, n, slot=slot):
                q = lists[slot, 1, s] - (8 - slot) * blocks
                return add(q, slot * blocks + lists[slot, 0, s], (q >= 0) & (q < blocks), n)

            total = jnp.where(present(slot), lists[slot, 2, 0], 0)
            n = lax.fori_loop(0, total, their_pair, n)

    def own_block(block, _):
        prepare_own(block, geo_ref, gx, gy, *own)
        return 0

    lax.fori_loop(0, blocks, own_block, 0)
    out_ref[...] = jnp.zeros_like(out_ref)
    for slot in range(9):
        for block in range(blocks):
            load(slot, block).wait()

    def entry(i):
        inside = i < n
        index = jnp.where(inside, todo[jnp.where(inside, i, 0)], 4 * blocks)
        a = index // near
        return a, index - a * near, jnp.where(inside, count_of[index], 0).astype(jnp.float32)

    def product_part(c, a, b, times, tile):
        first = pl.multiple_of(a * BLOCK + c * PART, PART)
        here = jnp.dot(tile[pl.ds(c * PART, PART), :], pan_all[b], preferred_element_type=jnp.float32)
        out_ref[pl.ds(first, PART), :] += times * here

    def ready_item(i, _):
        a, b, times = entry(i)
        fetch(i).wait()
        for c in range(BLOCK // PART):
            product_part(c, a, b, times, stored.at[lax.rem(i, depth)])

        @pl.when(i + depth < ready)
        def _():
            fetch(i + depth).start()

        return 0

    lax.fori_loop(0, ready, ready_item, 0)
    feat_load.wait()

    @pl.when(n > ready)
    def _():
        a0, b0, _ = entry(ready)
        for c in range(BLOCK // PART):
            align_part(c, a0, b0, own, feats, work0)
        tile1[...] = jnp.zeros_like(tile1)

        def two_items(j, before):
            i = ready + 2 * j
            for half, now, later, tile, past in (
                (0, work0, work1, tile0, tile1), (1, work1, work0, tile1, tile0)):
                a, b, times = entry(i + half)
                a_next, b_next, _ = entry(i + half + 1)
                for c in range(BLOCK // PART):
                    align_part(c, a_next, b_next, own, feats, later)
                sum_a, sum_b, sum_times = before
                product[...] = jnp.dot(past[...], pan_all[sum_b], preferred_element_type=jnp.float32)
                for c in range(BLOCK // PART):
                    tile_part(c, now, tile)
                out_ref[pl.ds(pl.multiple_of(sum_a * BLOCK, BLOCK), BLOCK), :] += sum_times * product[...]
                before = (a, b, times)
            return before

        last = lax.fori_loop(0, (n - ready + 1) // 2, two_items, (jnp.int32(0), jnp.int32(4 * blocks), jnp.float32(0)))
        for c in range(BLOCK // PART):
            product_part(c, *last, tile1)


def shards(nx, ny, geometry, panel, pair_first, pair_second, pair_count):
    fil, width = panel.shape
    blocks = fil // BLOCK
    near = 9 * blocks
    pair_len = pair_first.shape[0]
    long = -(-pair_len // 128) * 128
    made = 4 * (-(-pair_len // 4))
    table = jnp.pad(jnp.stack([pair_first, pair_second, jnp.broadcast_to(pair_count, (pair_len,))]),
                    ((0, 5), (0, long - pair_len)))
    items = CHUNKS + 2
    anywhere = pl.BlockSpec(memory_space=pl.ANY)
    vmem = pl.BlockSpec(memory_space=pltpu.VMEM)
    smem = pl.BlockSpec(memory_space=pltpu.SMEM)
    square = (BLOCK, BLOCK)
    lists, pans, tiles, feats = pl.pallas_call(
        functools.partial(halo_kernel, nx, ny),
        out_shape=(
            jax.ShapeDtypeStruct((9, 8, long), jnp.int32),
            jax.ShapeDtypeStruct((9, fil, width), jnp.bfloat16),
            jax.ShapeDtypeStruct((made,) + square, jnp.bfloat16),
            jax.ShapeDtypeStruct((near, 128, BLOCK), jnp.bfloat16),
        ),
        in_specs=[anywhere, smem, vmem, anywhere],
        out_specs=(anywhere, anywhere, anywhere, vmem),
        scratch_shapes=[
            pltpu.VMEM((9, 8, fil), jnp.float32),
            pltpu.VMEM((blocks, BLOCK, 32), jnp.bfloat16),
            pltpu.VMEM((blocks, BLOCK, 16), jnp.bfloat16),
            pltpu.VMEM((blocks, BLOCK, 80), jnp.bfloat16),
            pltpu.VMEM(square, jnp.float32),
            pltpu.VMEM(square, jnp.float32),
            pltpu.VMEM(square, jnp.float32),
            pltpu.VMEM(square, jnp.float32),
            pltpu.VMEM(square, jnp.bfloat16),
            pltpu.VMEM(square, jnp.bfloat16),
            pltpu.VMEM(square, jnp.bfloat16),
            pltpu.VMEM(square, jnp.bfloat16),
            pltpu.SemaphoreType.DMA((items,)),
            pltpu.SemaphoreType.DMA((items,)),
            pltpu.SemaphoreType.DMA((items,)),
            pltpu.SemaphoreType.DMA((items,)),
            pltpu.SemaphoreType.DMA((3, 2, items)),
            pltpu.SemaphoreType.DMA((3, 2, items)),
            pltpu.SemaphoreType.DMA((4, 4)),
        ],
        compiler_params=pltpu.CompilerParams(
            collective_id=0, has_side_effects=True, vmem_limit_bytes=VMEM_LIMIT),
        name="halo",
    )(table, table, geometry, panel)

    depth = 4
    return pl.pallas_call(
        functools.partial(product_kernel, nx, ny),
        out_shape=jax.ShapeDtypeStruct((fil, width), jnp.float32),
        in_specs=[smem, smem, vmem, anywhere, anywhere, anywhere, anywhere],
        out_specs=vmem,
        scratch_shapes=[
            pltpu.SMEM((blocks * near + 8,), jnp.int32),
            pltpu.SMEM((blocks * near + 8,), jnp.int32),
            pltpu.SMEM((blocks * near + 8,), jnp.int32),
            pltpu.VMEM((blocks, BLOCK, 32), jnp.bfloat16),
            pltpu.VMEM((blocks, BLOCK, 16), jnp.bfloat16),
            pltpu.VMEM((blocks, BLOCK, 80), jnp.bfloat16),
            pltpu.VMEM((near, 128, BLOCK), jnp.bfloat16),
            pltpu.VMEM((near, BLOCK, width), jnp.bfloat16),
            pltpu.VMEM(square, jnp.float32),
            pltpu.VMEM(square, jnp.float32),
            pltpu.VMEM(square, jnp.float32),
            pltpu.VMEM(square, jnp.float32),
            pltpu.VMEM(square, jnp.bfloat16),
            pltpu.VMEM(square, jnp.bfloat16),
            pltpu.VMEM((BLOCK, width), jnp.float32),
            pltpu.VMEM((depth,) + square, jnp.bfloat16),
            pltpu.SemaphoreType.DMA((9, blocks)),
            pltpu.SemaphoreType.DMA((depth,)),
            pltpu.SemaphoreType.DMA,
        ],
        compiler_params=pltpu.CompilerParams(vmem_limit_bytes=VMEM_LIMIT),
        name="products",
    )(table, lists, geometry, feats, panel, pans, tiles)


def solution(mesh):
    nx, ny = mesh.shape["gx"], mesh.shape["gy"]
    in_specs = (
        P(None, ("gx", "gy")),
        P(("gx", "gy"), None),
        P(("gx", "gy")),
        P(("gx", "gy")),
        P(("gx", "gy")),
    )
    out_specs = P(("gx", "gy"), None)
    return jax.shard_map(functools.partial(shards, nx, ny), mesh=mesh, in_specs=in_specs,
                         out_specs=out_specs, check_vma=False)
```

```python
import functools

import jax
import jax.numpy as jnp
from jax import lax
from jax.experimental import pallas as pl
from jax.experimental.pallas import tpu as pltpu
from jax.sharding import PartitionSpec as P

BLOCK = 512
CHUNKS = 4
PART = 512
GRID = 16.0
MESH = pl.DeviceIdType.MESH
VMEM_LIMIT = 56 * 1024 * 1024


def split(value):
    high = value.astype(jnp.bfloat16).astype(jnp.float32)
    return high, value - high


def features(geo, gx, gy, own):
    kind = lax.broadcasted_iota(jnp.int32, geo.shape, 0)
    place = kind < 3
    centre = jnp.where(kind == 0, gx.astype(jnp.float32) + 0.5, jnp.where(kind == 1, gy.astype(jnp.float32) + 0.5, 4.0))
    local = geo - centre
    coarse = jnp.where(place, jnp.floor(local * GRID + 0.5) * (1.0 / GRID), 0.0)
    fine = jnp.where(place, local - coarse, 0.0)
    radius = jnp.where(kind == 7, geo, 0.0)
    fine_high, rest = split(fine)
    fine_mid, fine_low = split(rest)
    both_high, both_low = split(fine + radius)
    norm = jnp.broadcast_to(jnp.sum(coarse * coarse, axis=0, keepdims=True), geo.shape)
    extra = jnp.broadcast_to(jnp.sum((2.0 * coarse + fine) * fine + radius * radius, axis=0, keepdims=True), geo.shape)
    norm_high, norm_low = split(norm)
    extra_high, rest = split(extra)
    extra_mid, extra_low = split(rest)
    direction = jnp.where((kind >= 3) & (kind <= 5), geo * geo[6:7, :], 0.0)
    blank = jnp.zeros_like(geo)
    if own:
        high, low = split(direction * BLOCK ** (-0.5))
        norms = jnp.where(kind == 0, norm_high, jnp.where(kind == 1, norm_low, jnp.where(kind <= 3, 1.0, 0.0)))
        extras = jnp.where(kind == 0, extra_high, jnp.where(kind == 1, extra_mid, jnp.where(
            kind == 2, extra_low, jnp.where(kind <= 5, 1.0, 0.0))))
        groups = [high, high, low, blank, coarse, norms, both_high, both_high, both_low,
                  coarse, coarse, coarse, fine_high, fine_mid, fine_low, extras]
    else:
        high, low = split(direction)
        sign = jnp.where(place, -2.0, 2.0)
        norms = jnp.where(kind <= 1, 1.0, jnp.where(kind == 2, norm_high, jnp.where(kind == 3, norm_low, 0.0)))
        extras = jnp.where(kind <= 2, 1.0, jnp.where(kind == 3, extra_high, jnp.where(
            kind == 4, extra_mid, jnp.where(kind == 5, extra_low, 0.0))))
        double = -2.0 * coarse
        groups = [high, low, high, blank, double, norms, sign * both_high, sign * both_low, sign * both_high,
                  -2.0 * fine_high, -2.0 * fine_mid, -2.0 * fine_low, double, double, double, extras]
    return jnp.concatenate(groups, axis=0)


def prepare_own(block, geo_ref, gx, gy, own_along, own_coarse, own_fine):
    lanes = pl.ds(pl.multiple_of(block * BLOCK, BLOCK), BLOCK)
    turned = features(geo_ref[:, lanes], gx, gy, True).T.astype(jnp.bfloat16)
    own_along[block] = turned[:, 0:32]
    own_coarse[block] = turned[:, 32:48]
    own_fine[block] = turned[:, 48:128]


def align_part(c, a, b, own, feats, work):
    own_along, own_coarse, own_fine = own
    aligned, square = work
    here = pl.ds(c * PART, PART)
    aligned[here, :] = jnp.dot(own_along[a, here, :], feats[b, 0:32, :], preferred_element_type=jnp.float32)
    square[here, :] = jnp.dot(
        own_coarse[a, here, :], feats[b, 32:48, :], preferred_element_type=jnp.float32
    ) + jnp.dot(own_fine[a, here, :], feats[b, 48:128, :], preferred_element_type=jnp.float32)


def tile_part(c, work, tile):
    aligned, square = work
    for r in range(c * PART, (c + 1) * PART, 16):
        here = pl.ds(r, 16)
        tile[here, :] = (aligned[here, :] * lax.rsqrt(square[here, :])).astype(jnp.bfloat16)


def halo_kernel(nx, ny, table_ref, list_ref, geo_ref, pan_ref, lists, pans, tiles, feats,
                geos, own_along, own_coarse, own_fine, aligned0, aligned1, square0, square1, tile0, tile1, tile2, tile3,
                x_send, x_recv, z_send, z_recv, y_send, y_recv, out_sems):
    own = own_along, own_coarse, own_fine
    work0, work1 = (aligned0, square0), (aligned1, square1)
    gx = lax.axis_index("gx")
    gy = lax.axis_index("gy")
    fil = pan_ref.shape[0]
    step = fil // CHUNKS
    items = CHUNKS + 2
    blocks = fil // BLOCK
    rounds = tiles.shape[0] // 4
    odd = lax.rem(gx, 2)
    partner = gx + 1 - 2 * odd
    relay_to = gx + 2 - 4 * odd
    relay_from = gx - 2 + 4 * odd
    has_to = (relay_to >= 0) & (relay_to < nx)
    has_from = (relay_from >= 0) & (relay_from < nx)
    has_up = gy + 1 < ny
    has_down = gy >= 1
    near_row = 2 - 2 * odd
    far_row = 2 * odd

    def part(k, own, row, col):
        if k == 0:
            return list_ref if own else lists.at[row * 3 + col]
        if k == 1:
            return geo_ref if own else geos.at[row * 3 + col]
        rows = pl.ds((k - 2) * step, step)
        return pan_ref.at[rows] if own else pans.at[row * 3 + col, rows]

    def x_copy(k):
        return pltpu.make_async_remote_copy(
            src_ref=part(k, True, 1, 1), dst_ref=part(k, False, far_row, 1),
            send_sem=x_send.at[k], recv_sem=x_recv.at[k],
            device_id=(partner, gy), device_id_type=MESH)

    def x_arrival(k):
        return pltpu.make_async_remote_copy(
            src_ref=part(k, True, 1, 1), dst_ref=part(k, False, near_row, 1),
            send_sem=x_send.at[k], recv_sem=x_recv.at[k],
            device_id=(partner, gy), device_id_type=MESH)

    def z_copy(k):
        return pltpu.make_async_remote_copy(
            src_ref=part(k, False, near_row, 1), dst_ref=part(k, False, far_row, 1),
            send_sem=z_send.at[k], recv_sem=z_recv.at[k],
            device_id=(relay_to, gy), device_id_type=MESH)

    def y_copy(k, kind, up):
        row = (1, near_row, far_row)[kind]
        return pltpu.make_async_remote_copy(
            src_ref=part(k, kind == 0, row, 1), dst_ref=part(k, False, row, 0 if up else 2),
            send_sem=y_send.at[kind, 1 if up else 0, k], recv_sem=y_recv.at[kind, 1 if up else 0, k],
            device_id=(gx, gy + 1 if up else gy - 1), device_id_type=MESH)

    def y_arrival(k, kind, up):
        row = (1, near_row, far_row)[kind]
        return pltpu.make_async_remote_copy(
            src_ref=part(k, kind == 0, row, 1), dst_ref=part(k, False, row, 0 if up else 2),
            send_sem=y_send.at[kind, 1 if up else 0, k], recv_sem=y_recv.at[kind, 1 if up else 0, k],
            device_id=(gx, gy - 1 if up else gy + 1), device_id_type=MESH)

    barrier = pltpu.get_barrier_semaphore()

    def greet(target, there):
        @pl.when(there)
        def _():
            pl.semaphore_signal(barrier, inc=1, device_id=target, device_id_type=MESH)

    pl.semaphore_signal(barrier, inc=1, device_id=(partner, gy), device_id_type=MESH)
    greet((relay_to, gy), has_to)
    greet((relay_from, gy), has_from)
    greet((gx, gy + 1), has_up)
    greet((gx, gy - 1), has_down)
    total = 1
    for there in (has_to, has_from, has_up, has_down):
        total = total + jnp.where(there, 1, 0)
    pl.semaphore_wait(barrier, total)

    def y_starts(k, kind):
        @pl.when(has_up)
        def _():
            y_copy(k, kind, True).start()

        @pl.when(has_down)
        def _():
            y_copy(k, kind, False).start()

    for k in range(2):
        x_copy(k).start()
        y_starts(k, 0)
    def relay(k):
        x_arrival(k).wait_recv()

        @pl.when(has_to)
        def _():
            z_copy(k).start()

        y_starts(k, 1)

    def spread(k):
        @pl.when(has_from)
        def _():
            z_copy(k).wait_recv()
            y_starts(k, 2)

    def own_block(block, _):
        prepare_own(block, geo_ref, gx, gy, *own)
        lanes = pl.ds(pl.multiple_of(block * BLOCK, BLOCK), BLOCK)
        feats[4 * blocks + block] = features(geo_ref[:, lanes], gx, gy, False).astype(jnp.bfloat16)
        return 0

    lax.fori_loop(0, blocks, own_block, 0)
    for k in range(2):
        relay(k)
    for k in range(2, items):
        x_copy(k).start()
    for k in range(2):
        spread(k)
    for k in range(2, items):
        y_starts(k, 0)

    def near_blocks(slot):
        def near_block(block, _):
            lanes = pl.ds(pl.multiple_of(block * BLOCK, BLOCK), BLOCK)
            feats[slot * blocks + block] = features(geos[slot, :, lanes], gx, gy, False).astype(jnp.bfloat16)
            return 0

        lax.fori_loop(0, blocks, near_block, 0)

    near_blocks(near_row * 3 + 1)

    @pl.when(has_from)
    def _():
        near_blocks(far_row * 3 + 1)

    def y_gets(kind, up):
        gets = has_down if up else has_up
        return gets & has_from if kind == 2 else gets

    for kind in range(3):
        for up in (True, False):
            @pl.when(y_gets(kind, up))
            def _():
                y_arrival(1, kind, up).wait_recv()
                near_blocks((1, near_row, far_row)[kind] * 3 + (0 if up else 2))

    def slot_ids(s):
        return list_ref[0, s], list_ref[1, s]

    piece = BLOCK // 4

    def out_copies(which, tile, s):
        return [pltpu.make_async_copy(tile.at[pl.ds(c * piece, piece)], tiles.at[s, pl.ds(c * piece, piece)],
                                      out_sems.at[which, c]) for c in range(4)]

    a0, b0 = slot_ids(0)
    for c in range(BLOCK // PART):
        align_part(c, a0, b0, own, feats, work0)

    events = {}
    for c, at in enumerate((0, 1, 3, 5)):
        events.setdefault(at * rounds // 12, []).append((relay, c + 2))
    for c, at in enumerate((2, 4, 6, 8)):
        events.setdefault(at * rounds // 12, []).append((spread, c + 2))
    held = tile0, tile1, tile2, tile3

    def round_step(i, _):
        for at, calls in events.items():
            @pl.when(i == at)
            def _():
                for call, k in calls:
                    call(k)

        for which, tile in enumerate(held):
            now, later = (work0, work1) if which % 2 == 0 else (work1, work0)
            s = 4 * i + which
            a_next, b_next = slot_ids(jnp.minimum(s + 1, 4 * rounds - 1))

            @pl.when(i > 0)
            def _():
                for copy in out_copies(which, tile, s):
                    copy.wait()

            align_part(0, a_next, b_next, own, feats, later)
            tile_part(0, now, tile)
            for copy in out_copies(which, tile, s):
                copy.start()
        return 0

    lax.fori_loop(0, rounds, round_step, 0)
    for which, tile in enumerate(held):
        for copy in out_copies(which, tile, 4 * rounds - 4 + which):
            copy.wait()

    for k in range(items):
        x_copy(k).wait_send()

        @pl.when(has_to)
        def _():
            z_copy(k).wait_send()

        for kind in range(3):
            for up, sends, gets in ((True, has_up, has_down), (False, has_down, has_up)):
                if kind == 2:
                    sends = sends & has_from
                    gets = gets & has_from

                @pl.when(sends)
                def _():
                    y_copy(k, kind, up).wait_send()

                if k != 1:
                    @pl.when(gets)
                    def _():
                        y_arrival(k, kind, up).wait_recv()


def product_kernel(nx, ny, list_ref, lists, geo_ref, feats_ref, pan_ref, pans, tiles,
                   out_ref, count_of, todo, slot_of, own_along, own_coarse, own_fine, feats, pan_all,
                   aligned0, aligned1, square0, square1, tile0, tile1, product, stored, sems, stored_sems, feat_sem):
    own = own_along, own_coarse, own_fine
    work0, work1 = (aligned0, square0), (aligned1, square1)
    gx = lax.axis_index("gx")
    gy = lax.axis_index("gy")
    fil, width = pan_ref.shape
    blocks = fil // BLOCK
    near = 9 * blocks
    spare = blocks * near
    sides = [(sx, sy) for sx in range(3) for sy in range(3)]

    def present(slot):
        sx, sy = sides[slot]
        there = (gx + (sx - 1) >= 0) & (gx + (sx - 1) < nx)
        return there & (gy + (sy - 1) >= 0) & (gy + (sy - 1) < ny)

    def load(slot, block):
        source = pan_ref.at[pl.ds(block * BLOCK, BLOCK)] if slot == 4 else pans.at[slot, pl.ds(block * BLOCK, BLOCK)]
        return pltpu.make_async_copy(source, pan_all.at[slot * blocks + block], sems.at[slot, block])

    feat_load = pltpu.make_async_copy(feats_ref, feats, feat_sem)
    for slot in (4, 0, 1, 2, 3, 5, 6, 7, 8):
        for block in range(blocks):
            load(slot, block).start()
    feat_load.start()

    def clear(i, _):
        count_of[i] = 0
        return 0

    lax.fori_loop(0, spare + 8, clear, 0, unroll=8)

    def add(a, b, wanted, n):
        where_ = jnp.where(wanted, a * near + b, spare)
        seen = count_of[where_]
        todo[n] = where_
        count_of[where_] = seen + 1
        return n + jnp.where(wanted & (seen == 0), 1, 0)

    def own_pair(s, n):
        slot_of[n] = s
        return add(list_ref[0, s], list_ref[1, s], True, n)

    made = jnp.minimum(list_ref[2, 0], tiles.shape[0])
    ready = lax.fori_loop(0, made, own_pair, 0)
    depth = stored.shape[0]

    def fetch(i):
        slot = lax.rem(i, depth)
        return pltpu.make_async_copy(tiles.at[slot_of[i]], stored.at[slot], stored_sems.at[slot])

    for i in range(depth):
        @pl.when(i < ready)
        def _():
            fetch(i).start()

    def mirrored(s, n):
        q = list_ref[1, s] - 4 * blocks
        a = list_ref[0, s]
        return add(q, 4 * blocks + a, (q >= 0) & (q < blocks) & (q != a), n)

    def late_pair(s, n):
        return add(list_ref[0, s], list_ref[1, s], True, n)

    n = lax.fori_loop(made, list_ref[2, 0], late_pair, ready)
    n = lax.fori_loop(0, list_ref[2, 0], mirrored, n)
    for slot in range(9):
        if slot != 4:
            def their_pair(s, n, slot=slot):
                q = lists[slot, 1, s] - (8 - slot) * blocks
                return add(q, slot * blocks + lists[slot, 0, s], (q >= 0) & (q < blocks), n)

            total = jnp.where(present(slot), lists[slot, 2, 0], 0)
            n = lax.fori_loop(0, total, their_pair, n)

    def own_block(block, _):
        prepare_own(block, geo_ref, gx, gy, *own)
        return 0

    lax.fori_loop(0, blocks, own_block, 0)
    out_ref[...] = jnp.zeros_like(out_ref)
    for slot in range(9):
        for block in range(blocks):
            load(slot, block).wait()

    def entry(i):
        inside = i < n
        index = jnp.where(inside, todo[jnp.where(inside, i, 0)], 4 * blocks)
        a = index // near
        return a, index - a * near, jnp.where(inside, count_of[index], 0).astype(jnp.float32)

    def product_part(c, a, b, times, tile):
        first = pl.multiple_of(a * BLOCK + c * PART, PART)
        here = jnp.dot(tile[pl.ds(c * PART, PART), :], pan_all[b], preferred_element_type=jnp.float32)
        out_ref[pl.ds(first, PART), :] += times * here

    def ready_item(i, _):
        a, b, times = entry(i)
        fetch(i).wait()
        for c in range(BLOCK // PART):
            product_part(c, a, b, times, stored.at[lax.rem(i, depth)])

        @pl.when(i + depth < ready)
        def _():
            fetch(i + depth).start()

        return 0

    lax.fori_loop(0, ready, ready_item, 0)
    feat_load.wait()

    @pl.when(n > ready)
    def _():
        a0, b0, _ = entry(ready)
        for c in range(BLOCK // PART):
            align_part(c, a0, b0, own, feats, work0)
        tile1[...] = jnp.zeros_like(tile1)

        def two_items(j, before):
            i = ready + 2 * j
            for half, now, later, tile, past in (
                (0, work0, work1, tile0, tile1), (1, work1, work0, tile1, tile0)):
                a, b, times = entry(i + half)
                a_next, b_next, _ = entry(i + half + 1)
                for c in range(BLOCK // PART):
                    align_part(c, a_next, b_next, own, feats, later)
                sum_a, sum_b, sum_times = before
                product[...] = jnp.dot(past[...], pan_all[sum_b], preferred_element_type=jnp.float32)
                for c in range(BLOCK // PART):
                    tile_part(c, now, tile)
                out_ref[pl.ds(pl.multiple_of(sum_a * BLOCK, BLOCK), BLOCK), :] += sum_times * product[...]
                before = (a, b, times)
            return before

        last = lax.fori_loop(0, (n - ready + 1) // 2, two_items, (jnp.int32(0), jnp.int32(4 * blocks), jnp.float32(0)))
        for c in range(BLOCK // PART):
            product_part(c, *last, tile1)


def shards(nx, ny, geometry, panel, pair_first, pair_second, pair_count):
    fil, width = panel.shape
    blocks = fil // BLOCK
    near = 9 * blocks
    pair_len = pair_first.shape[0]
    long = -(-pair_len // 128) * 128
    made = 4 * (-(-3 * pair_len // 16))
    table = jnp.pad(jnp.stack([pair_first, pair_second, jnp.broadcast_to(pair_count, (pair_len,))]),
                    ((0, 5), (0, long - pair_len)))
    items = CHUNKS + 2
    anywhere = pl.BlockSpec(memory_space=pl.ANY)
    vmem = pl.BlockSpec(memory_space=pltpu.VMEM)
    smem = pl.BlockSpec(memory_space=pltpu.SMEM)
    square = (BLOCK, BLOCK)
    lists, pans, tiles, feats = pl.pallas_call(
        functools.partial(halo_kernel, nx, ny),
        out_shape=(
            jax.ShapeDtypeStruct((9, 8, long), jnp.int32),
            jax.ShapeDtypeStruct((9, fil, width), jnp.bfloat16),
            jax.ShapeDtypeStruct((made,) + square, jnp.bfloat16),
            jax.ShapeDtypeStruct((near, 128, BLOCK), jnp.bfloat16),
        ),
        in_specs=[anywhere, smem, vmem, anywhere],
        out_specs=(anywhere, anywhere, anywhere, vmem),
        scratch_shapes=[
            pltpu.VMEM((9, 8, fil), jnp.float32),
            pltpu.VMEM((blocks, BLOCK, 32), jnp.bfloat16),
            pltpu.VMEM((blocks, BLOCK, 16), jnp.bfloat16),
            pltpu.VMEM((blocks, BLOCK, 80), jnp.bfloat16),
            pltpu.VMEM(square, jnp.float32),
            pltpu.VMEM(square, jnp.float32),
            pltpu.VMEM(square, jnp.float32),
            pltpu.VMEM(square, jnp.float32),
            pltpu.VMEM(square, jnp.bfloat16),
            pltpu.VMEM(square, jnp.bfloat16),
            pltpu.VMEM(square, jnp.bfloat16),
            pltpu.VMEM(square, jnp.bfloat16),
            pltpu.SemaphoreType.DMA((items,)),
            pltpu.SemaphoreType.DMA((items,)),
            pltpu.SemaphoreType.DMA((items,)),
            pltpu.SemaphoreType.DMA((items,)),
            pltpu.SemaphoreType.DMA((3, 2, items)),
            pltpu.SemaphoreType.DMA((3, 2, items)),
            pltpu.SemaphoreType.DMA((4, 4)),
        ],
        compiler_params=pltpu.CompilerParams(
            collective_id=0, has_side_effects=True, vmem_limit_bytes=VMEM_LIMIT),
        name="halo",
    )(table, table, geometry, panel)

    depth = 4
    return pl.pallas_call(
        functools.partial(product_kernel, nx, ny),
        out_shape=jax.ShapeDtypeStruct((fil, width), jnp.float32),
        in_specs=[smem, smem, vmem, anywhere, anywhere, anywhere, anywhere],
        out_specs=vmem,
        scratch_shapes=[
            pltpu.SMEM((blocks * near + 8,), jnp.int32),
            pltpu.SMEM((blocks * near + 8,), jnp.int32),
            pltpu.SMEM((blocks * near + 8,), jnp.int32),
            pltpu.VMEM((blocks, BLOCK, 32), jnp.bfloat16),
            pltpu.VMEM((blocks, BLOCK, 16), jnp.bfloat16),
            pltpu.VMEM((blocks, BLOCK, 80), jnp.bfloat16),
            pltpu.VMEM((near, 128, BLOCK), jnp.bfloat16),
            pltpu.VMEM((near, BLOCK, width), jnp.bfloat16),
            pltpu.VMEM(square, jnp.float32),
            pltpu.VMEM(square, jnp.float32),
            pltpu.VMEM(square, jnp.float32),
            pltpu.VMEM(square, jnp.float32),
            pltpu.VMEM(square, jnp.bfloat16),
            pltpu.VMEM(square, jnp.bfloat16),
            pltpu.VMEM((BLOCK, width), jnp.float32),
            pltpu.VMEM((depth,) + square, jnp.bfloat16),
            pltpu.SemaphoreType.DMA((9, blocks)),
            pltpu.SemaphoreType.DMA((depth,)),
            pltpu.SemaphoreType.DMA,
        ],
        compiler_params=pltpu.CompilerParams(vmem_limit_bytes=VMEM_LIMIT),
        name="products",
    )(table, lists, geometry, feats, panel, pans, tiles)


def solution(mesh):
    nx, ny = mesh.shape["gx"], mesh.shape["gy"]
    in_specs = (
        P(None, ("gx", "gy")),
        P(("gx", "gy"), None),
        P(("gx", "gy")),
        P(("gx", "gy")),
        P(("gx", "gy")),
    )
    out_specs = P(("gx", "gy"), None)
    return jax.shard_map(functools.partial(shards, nx, ny), mesh=mesh, in_specs=in_specs,
                         out_specs=out_specs, check_vma=False)
```
